32 devices in a mesh: seq: 16 (over z, y, x), dp: 2 (over core).
Axes of the slice: x: 2, y: 2, z: 4, core: 2. Of those that a mesh axis runs over, the one named last changes fastest.
Arguments:
- queries: bfloat16 [2, 4096, 1024], P('dp', 'seq'), may hold values from -1000 to 1000, as said below
- key_rows: bfloat16 [2, 4096, 1024], P('dp', 'seq'), may hold values from -1000 to 1000, as said below
- value_rows: bfloat16 [2, 4096, 1024], P('dp', 'seq'), may hold values from -6 to 6
- cotangent: bfloat16 [2, 4096, 1024], P('dp', 'seq'), may hold values from -6 to 6
- w_out: bfloat16 [1024, 1024], P('dp'), may hold values from -0.1875 to 0.1875
- cluster_ids: int32 [2, 4096], P('dp', 'seq'), may hold values from 0 to 63, as said below
Outputs:
- projected: bfloat16 [2, 4096, 1024], P('dp', 'seq')
- grad_queries: bfloat16 [2, 4096, 1024], P('dp', 'seq')
- grad_keys: bfloat16 [2, 4096, 1024], P('dp', 'seq')
- grad_values: bfloat16 [2, 4096, 1024], P('dp', 'seq')
- weight_grad: float32 [1024, 1024], P(('seq', 'dp'))
The draws below stay inside these ranges and needn't reach their ends.
Inputs may be any that keep to these rules, and one draw needn't show every extreme that they name: `cluster_ids`: among the 256 tokens of one index of seq no cluster id occurs more than 8 times; in every sequence some cluster has exactly 8 tokens on every index of seq. `queries`: finite values. `key_rows`: finite values.
All inputs are finite; a program needn't handle non-finite values.
Results may differ from the reference program's by a relative error of at most 0.014.
Values may be sent and summed in bfloat16 or wider, within the bound.
A program may use at most 128 MiB of HBM per device.

```python
import math
import jax
import jax.numpy as jnp
from jax import lax

HEADS = 8
HD = 128
DOUT = 1024
CL_DEV = 4
TOK_DEV = 256
HW = 1024
CLUSTERS = 64
CAP = 8
BLOCK = 128
LEN = 4096
SEQS = 2
ALL = 8192


def scaled_rows(key):
    key_noise = jax.random.fold_in(key, 1)
    key_scale = jax.random.fold_in(key, 2)
    key_column = jax.random.fold_in(key, 3)
    noise = jax.random.normal(key_noise, (SEQS, LEN, HEADS, HD), jnp.float32)
    row_scale = jnp.exp(jax.random.uniform(key_scale, (SEQS, LEN, HEADS, 1), jnp.float32, 0.0, math.log(10.0)))
    column_scale = jnp.exp(jax.random.uniform(key_column, (HEADS, HD), jnp.float32, 0.0, math.log(10.0)))
    noise = jnp.clip(noise, -6.0, 6.0)
    return (noise * row_scale * column_scale).reshape(SEQS, LEN, HW)


def draw_queries(key, part):
    return scaled_rows(jax.random.fold_in(key, 11)).astype(jnp.bfloat16)


def draw_key_rows(key, part):
    return scaled_rows(jax.random.fold_in(key, 23)).astype(jnp.bfloat16)


def draw_cluster_ids(key, part):
    devices = LEN // TOK_DEV
    clusters = CL_DEV * devices
    capacity = 2 * TOK_DEV // clusters
    total_slots = clusters * capacity
    base = jax.random.fold_in(key, 37)
    full_base = jax.random.fold_in(base, 1)
    dev_base = jax.random.fold_in(base, 2)
    seq_index = jnp.arange(SEQS, dtype=jnp.int32)
    dev_index = jnp.arange(devices, dtype=jnp.int32)

    def fullest_of(seq_number):
        return jax.random.randint(jax.random.fold_in(full_base, seq_number), (), 0, clusters)
    fullest = jax.vmap(fullest_of)(seq_index)

    def one_device(seq_number, dev_number, offset):
        sub = jax.random.fold_in(jax.random.fold_in(dev_base, seq_number), dev_number)
        key_pick = jax.random.fold_in(sub, 1)
        key_order = jax.random.fold_in(sub, 2)
        forced = jnp.arange(capacity, dtype=jnp.int32)
        others = capacity + jax.random.permutation(key_pick, total_slots - capacity)[:TOK_DEV - capacity].astype(jnp.int32)
        chosen = jnp.concatenate([forced, others])
        relative = chosen // capacity
        labels = (relative + offset) % clusters
        return jax.random.permutation(key_order, labels).astype(jnp.int32)

    def one_sequence(seq_number, offset):
        return jax.vmap(lambda dev_number: one_device(seq_number, dev_number, offset))(dev_index)
    labels = jax.vmap(one_sequence)(seq_index, fullest)
    return labels.reshape(SEQS, LEN).astype(jnp.int32)


def steps_of(stream_key, extent, split, smallest, high):
    gain, own = 1.0, jax.random.fold_in(stream_key, 6)
    for position, shards_of in split:
        heights = jnp.exp(jax.random.uniform(jax.random.fold_in(own, position), (shards_of,), jnp.float32, smallest / len(split), high / len(split)))
        gain = gain * jnp.repeat(heights, extent[position] // shards_of).reshape([-1 if axis == position else 1 for axis in range(len(extent))])
    return gain


def bell_draw(rng, dims, scale, bound, pieces=(), kind=jnp.bfloat16):
    gain = steps_of(rng, dims, pieces, -0.22, 0.18) if pieces else 1.0
    array = jax.random.normal(rng, dims, jnp.float32) * scale * gain
    return jnp.minimum(jnp.maximum(array, -bound), bound).astype(kind)


def setup_inputs(seed: int = 0) -> dict:
    arg_keys = jax.random.split(jax.random.key(seed), 7)
    return {
        "queries": draw_queries(jax.random.fold_in(arg_keys[6], 71), 0),
        "key_rows": draw_key_rows(jax.random.fold_in(arg_keys[6], 71), 0),
        "value_rows": bell_draw(arg_keys[2], (SEQS, LEN, HW), 1.0, 6.0, ((0, 2), (1, 16))),
        "cotangent": bell_draw(arg_keys[3], (SEQS, LEN, DOUT), 1.0, 6.0, ((0, 2), (1, 16))),
        "w_out": bell_draw(arg_keys[4], (HW, DOUT), HW ** -0.5, 0.1875, ((0, 2),)),
        "cluster_ids": draw_cluster_ids(jax.random.fold_in(arg_keys[6], 71), 0),
    }


EPS = 1e-06

def head_norm(matrix):
    shaped = matrix.astype(jnp.float32).reshape(matrix.shape[0], HW // HD, HD)
    factor = lax.rsqrt(lax.optimization_barrier(jnp.mean(shaped * shaped, axis=-1, keepdims=True)) + EPS)
    return (shaped * factor, factor)

def norm_back(gradient, normed, factor):
    shaped = gradient.astype(jnp.float32).reshape(normed.shape)
    inner = lax.optimization_barrier(jnp.mean(shaped * normed, axis=-1, keepdims=True))
    return (factor * (shaped - normed * inner)).reshape(normed.shape[0], HW)

def block_rows(cluster_row):
    grouped = cluster_row.reshape(LEN // TOK_DEV, TOK_DEV)
    matching = grouped[:, :, None] == grouped[:, None, :]
    positions = jnp.arange(TOK_DEV, dtype=jnp.int32)
    earlier = positions[None, :] < positions[:, None]
    ranks = lax.optimization_barrier(jnp.sum(jnp.logical_and(matching, earlier[None]), axis=2)).astype(jnp.int32)
    devices = jnp.arange(LEN // TOK_DEV, dtype=jnp.int32)[:, None]
    return (devices * CAP + ranks).reshape(LEN).astype(jnp.int32)

def split_heads(blocks):
    return blocks.reshape(blocks.shape[0], blocks.shape[1], HW // HD, HD).astype(jnp.float32)

def attend(q_blk, k_blk, v_blk, key_valid):
    q_four, k_four, v_four = (split_heads(q_blk), split_heads(k_blk), split_heads(v_blk))
    scores = jnp.einsum('cqhd,ckhd->chqk', q_four, k_four) / math.sqrt(HD)
    positions = jnp.arange(BLOCK)
    below_diag = positions[None, :] <= positions[:, None]
    on_diagonal = positions[None, :] == positions[:, None]
    allowed = jnp.logical_or(jnp.logical_and(key_valid[:, None, None, :], below_diag[None, None]), on_diagonal[None, None])
    weights = jnp.where(allowed, jnp.exp(scores), 0.0)
    probs = weights / lax.optimization_barrier(jnp.sum(weights, axis=-1, keepdims=True))
    probs_b = probs.astype(jnp.bfloat16)
    attn = jnp.einsum('chqk,ckhd->cqhd', probs_b.astype(jnp.float32), v_four).astype(jnp.bfloat16)
    return (attn.reshape(q_blk.shape), probs, probs_b)

def attend_back(q_blk, k_blk, v_blk, probs, probs_b, attn, d_blk):
    q_four, k_four, v_four = (split_heads(q_blk), split_heads(k_blk), split_heads(v_blk))
    d_four, a_four = (split_heads(d_blk), split_heads(attn))
    pb_float = probs_b.astype(jnp.float32)
    grad_value = jnp.einsum('chqk,cqhd->ckhd', pb_float, d_four).astype(jnp.bfloat16)
    grad_prob = jnp.einsum('cqhd,ckhd->chqk', d_four, v_four)
    delta_row = lax.optimization_barrier(jnp.sum(d_four * a_four, axis=-1))
    grad_score = (probs * (grad_prob - jnp.transpose(delta_row, (0, 2, 1))[..., None])).astype(jnp.bfloat16)
    gs_float = grad_score.astype(jnp.float32)
    grad_qhat = (jnp.einsum('chqk,ckhd->cqhd', gs_float, k_four) / math.sqrt(HD)).astype(jnp.bfloat16)
    grad_khat = (jnp.einsum('chqk,cqhd->ckhd', gs_float, q_four) / math.sqrt(HD)).astype(jnp.bfloat16)
    shape = q_blk.shape
    return (grad_qhat.reshape(shape), grad_khat.reshape(shape), grad_value.reshape(shape))

def one_sequence(w_out, inputs):
    queries, key_rows, value_rows, cotangent, cluster_row = inputs
    q_norm, q_factor = head_norm(queries)
    k_norm, k_factor = head_norm(key_rows)
    q_hat = q_norm.reshape(LEN, HW).astype(jnp.bfloat16)
    k_hat = k_norm.reshape(LEN, HW).astype(jnp.bfloat16)
    rows_of = block_rows(cluster_row)

    def place(matrix):
        empty = jnp.zeros((CLUSTERS, BLOCK, matrix.shape[1]), matrix.dtype)
        return empty.at[cluster_row, rows_of].set(matrix)

    def take(blocks):
        return blocks[cluster_row, rows_of]
    key_valid = jnp.zeros((CLUSTERS, BLOCK), jnp.bool_).at[cluster_row, rows_of].set(True)
    q_blk, k_blk, v_blk = (place(q_hat), place(k_hat), place(value_rows))
    attn_blk, probs, probs_b = attend(q_blk, k_blk, v_blk, key_valid)
    attn = take(attn_blk)
    projected = jnp.dot(attn, w_out, preferred_element_type=jnp.float32).astype(jnp.bfloat16)
    grad_attn = jnp.dot(cotangent, w_out.T, preferred_element_type=jnp.float32).astype(jnp.bfloat16)
    grad_qblk, grad_kblk, grad_vblk = attend_back(q_blk, k_blk, v_blk, probs, probs_b, attn_blk, place(grad_attn))
    grad_queries = norm_back(take(grad_qblk), q_norm, q_factor).astype(jnp.bfloat16)
    grad_keys = norm_back(take(grad_kblk), k_norm, k_factor).astype(jnp.bfloat16)
    grad_values = take(grad_vblk)
    weight_term = jnp.dot(attn.T, cotangent, preferred_element_type=jnp.float32)
    return (projected, grad_queries, grad_keys, grad_values, weight_term)

def reference(queries, key_rows, value_rows, cotangent, w_out, cluster_ids):
    results = lax.map(partial_sequence(w_out), (queries, key_rows, value_rows, cotangent, cluster_ids))
    projected, grad_queries, grad_keys, grad_values, weight_terms = results
    weight_grad = lax.optimization_barrier(jnp.sum(weight_terms, axis=0)) / math.sqrt(ALL)
    return (projected, grad_queries, grad_keys, grad_values, weight_grad)

def partial_sequence(w_out):

    def runner(inputs):
        return one_sequence(w_out, inputs)
    return runner
```

```python
import math

import jax
import jax.numpy as jnp
from jax import lax
from jax.sharding import PartitionSpec as P

HD = 128
CL_DEV = 4


EPS = 1e-06


def head_norm(matrix):
    shaped = matrix.astype(jnp.float32).reshape(matrix.shape[0], matrix.shape[1] // HD, HD)
    factor = lax.rsqrt(jnp.mean(shaped * shaped, axis=-1, keepdims=True) + EPS)
    return (shaped * factor, factor)


def norm_back(gradient, normed, factor):
    shaped = gradient.astype(jnp.float32).reshape(normed.shape)
    inner = jnp.mean(shaped * normed, axis=-1, keepdims=True)
    return (factor * (shaped - normed * inner)).reshape(normed.shape[0], -1)


def split_heads(blocks):
    return blocks.reshape(blocks.shape[0], blocks.shape[1], blocks.shape[2] // HD, HD)


def attend(q_blk, k_blk, v_blk, key_valid):
    q_four, k_four, v_four = (split_heads(q_blk), split_heads(k_blk), split_heads(v_blk))
    scores = jnp.einsum(
        "cqhd,ckhd->chqk", q_four, k_four, preferred_element_type=jnp.float32
    ) / math.sqrt(HD)
    positions = jnp.arange(q_blk.shape[1])
    below_diag = positions[None, :] <= positions[:, None]
    on_diagonal = positions[None, :] == positions[:, None]
    allowed = jnp.logical_or(
        jnp.logical_and(key_valid[:, None, None, :], below_diag[None, None]),
        on_diagonal[None, None],
    )
    weights = jnp.where(allowed, jnp.exp(scores), 0.0)
    probs = weights / jnp.sum(weights, axis=-1, keepdims=True)
    probs_b = probs.astype(jnp.bfloat16)
    attn = jnp.einsum(
        "chqk,ckhd->cqhd", probs_b, v_four, preferred_element_type=jnp.float32
    ).astype(jnp.bfloat16)
    return (attn.reshape(q_blk.shape), probs, probs_b)


def attend_back(q_blk, k_blk, v_blk, probs, probs_b, attn, d_blk):
    q_four, k_four, v_four = (split_heads(q_blk), split_heads(k_blk), split_heads(v_blk))
    d_four, a_four = (split_heads(d_blk), split_heads(attn))
    grad_value = jnp.einsum(
        "chqk,cqhd->ckhd", probs_b, d_four, preferred_element_type=jnp.float32
    ).astype(jnp.bfloat16)
    grad_prob = jnp.einsum("cqhd,ckhd->chqk", d_four, v_four, preferred_element_type=jnp.float32)
    delta_row = jnp.sum(d_four.astype(jnp.float32) * a_four.astype(jnp.float32), axis=-1)
    grad_score = (probs * (grad_prob - jnp.transpose(delta_row, (0, 2, 1))[..., None])).astype(
        jnp.bfloat16
    )
    grad_qhat = jnp.einsum(
        "chqk,ckhd->cqhd", grad_score, k_four, preferred_element_type=jnp.float32
    ) / math.sqrt(HD)
    grad_khat = jnp.einsum(
        "chqk,cqhd->ckhd", grad_score, q_four, preferred_element_type=jnp.float32
    ) / math.sqrt(HD)
    shape = q_blk.shape
    return (
        grad_qhat.astype(jnp.bfloat16).reshape(shape),
        grad_khat.astype(jnp.bfloat16).reshape(shape),
        grad_value.reshape(shape),
    )


def per_device_slots(queries, key_rows, value_rows, cotangent, w_out, cluster_ids):
    token_count = queries.shape[1]
    features = queries.shape[2]
    seq_devices = lax.axis_size("seq")
    data_devices = lax.axis_size("dp")
    capacity = 2 * token_count // (CL_DEV * seq_devices)
    total_slots = 2 * token_count
    labels = cluster_ids[0]
    positions = jnp.arange(token_count)
    matching = labels[:, None] == labels[None, :]
    earlier = positions[None, :] < positions[:, None]
    ranks = jnp.sum(jnp.logical_and(matching, earlier), axis=1)
    slot_index = labels * capacity + ranks

    def pack(matrix):
        empty = jnp.zeros((total_slots, matrix.shape[1]), matrix.dtype)
        return (
            empty.at[slot_index].set(matrix).reshape(seq_devices, CL_DEV, capacity, matrix.shape[1])
        )

    def unpack(returned):
        return returned.reshape(total_slots, -1)[slot_index]

    taken_slots = (
        jnp.zeros((total_slots,), jnp.bfloat16)
        .at[slot_index]
        .set(1.0)
        .reshape(seq_devices, CL_DEV, capacity)
    )
    q_norm, q_factor = head_norm(queries[0])
    k_norm, k_factor = head_norm(key_rows[0])
    q_hat = q_norm.reshape(token_count, features).astype(jnp.bfloat16)
    k_hat = k_norm.reshape(token_count, features).astype(jnp.bfloat16)
    cotan = cotangent[0]
    w_full = lax.all_gather(w_out, "dp", axis=0, tiled=True)
    received = (
        lax.all_to_all(pack(q_hat), "seq", split_axis=0, concat_axis=2, tiled=True),
        lax.all_to_all(pack(k_hat), "seq", split_axis=0, concat_axis=2, tiled=True),
        lax.all_to_all(pack(value_rows[0]), "seq", split_axis=0, concat_axis=2, tiled=True),
        lax.all_to_all(taken_slots, "seq", split_axis=0, concat_axis=2, tiled=True),
    )
    q_blk, k_blk, v_blk = (received[0][0], received[1][0], received[2][0])
    key_valid = received[3][0] > 0
    attn_blk, probs, probs_b = attend(q_blk, k_blk, v_blk, key_valid)
    attn_back = lax.all_to_all(attn_blk[None], "seq", split_axis=2, concat_axis=0, tiled=True)
    attn = unpack(attn_back)
    grad_attn = lax.dot_general(
        cotan, w_full, (((1,), (1,)), ((), ())), preferred_element_type=jnp.float32
    ).astype(jnp.bfloat16)
    grad_recv = lax.all_to_all(pack(grad_attn), "seq", split_axis=0, concat_axis=2, tiled=True)
    grad_qblk, grad_kblk, grad_vblk = attend_back(
        q_blk, k_blk, v_blk, probs, probs_b, attn_blk, grad_recv[0]
    )
    grads_back = (
        lax.all_to_all(grad_qblk[None], "seq", split_axis=2, concat_axis=0, tiled=True),
        lax.all_to_all(grad_kblk[None], "seq", split_axis=2, concat_axis=0, tiled=True),
        lax.all_to_all(grad_vblk[None], "seq", split_axis=2, concat_axis=0, tiled=True),
    )
    grad_qhat, grad_khat, grad_values = (
        unpack(grads_back[0]),
        unpack(grads_back[1]),
        unpack(grads_back[2]),
    )
    projected = jnp.dot(attn, w_full, preferred_element_type=jnp.float32).astype(jnp.bfloat16)
    grad_queries = norm_back(grad_qhat, q_norm, q_factor).astype(jnp.bfloat16)
    grad_keys = norm_back(grad_khat, k_norm, k_factor).astype(jnp.bfloat16)
    local_term = lax.dot_general(
        attn, cotan, (((0,), (0,)), ((), ())), preferred_element_type=jnp.float32
    )
    summed = lax.psum_scatter(local_term, ("seq", "dp"), scatter_dimension=0, tiled=True)
    weight_grad = summed / math.sqrt(token_count * seq_devices * data_devices)
    return (projected[None], grad_queries[None], grad_keys[None], grad_values[None], weight_grad)


def swap_cores(array):
    return lax.ppermute(array, "dp", [(0, 1), (1, 0)])


def per_device_heads(queries, key_rows, value_rows, cotangent, w_out, cluster_ids):
    tokens, features = queries.shape[1], queries.shape[2]
    heads = features // HD
    seq_devices = lax.axis_size("seq")
    half = tokens // 2
    clusters = CL_DEV * seq_devices
    capacity = 2 * tokens // clusters
    core = lax.axis_index("dp")
    other = 1 - core
    chip = lax.axis_index("seq")
    seq_here = chip // heads
    labels = cluster_ids[0]
    positions = jnp.arange(tokens)
    matching = labels[:, None] == labels[None, :]
    earlier = positions[None, :] < positions[:, None]
    ranks = jnp.sum(jnp.logical_and(matching, earlier), axis=1)
    slot_index = (labels * capacity + ranks).astype(jnp.int32)
    all_slots = lax.all_gather(slot_index, ("dp", "seq"), axis=0, tiled=False)
    all_slots = all_slots.reshape(2, seq_devices, tokens)
    slots = lax.dynamic_index_in_dim(all_slots, seq_here, 0, keepdims=False)
    my_slots = clusters * capacity // 2
    wanted = core * my_slots + jnp.arange(my_slots)
    one_hot = (slots[:, None, :] == wanted[None, :, None]).astype(jnp.bfloat16)

    def pick(array, index):
        return lax.dynamic_index_in_dim(array, index, 0, keepdims=False)

    def in_order(mine, theirs, index, axis):
        first = jnp.where(index == 0, mine, theirs)
        second = jnp.where(index == 0, theirs, mine)
        return jnp.stack([first, second], axis=axis)

    def dispatch(arrays):
        count = len(arrays)
        stacked = jnp.stack([a.reshape(2, half, heads, HD) for a in arrays], axis=3)
        stacked = jnp.transpose(stacked, (0, 2, 1, 3, 4)).reshape(2, heads, half, count * HD)
        theirs = swap_cores(pick(stacked, other))
        both = in_order(pick(stacked, core), theirs, core, 0)
        both = both.reshape(2 * heads, half, count * HD)
        landed = lax.all_to_all(both, "seq", split_axis=0, concat_axis=0, tiled=True)
        full = in_order(landed, swap_cores(landed), core, 1)
        full = full.reshape(seq_devices, tokens, count * HD)
        packed = jnp.einsum(
            "dst,dtf->dsf", one_hot, full, preferred_element_type=jnp.float32
        ).astype(jnp.bfloat16)
        packed = packed.reshape(seq_devices, clusters // 2, capacity, count * HD)
        packed = jnp.transpose(packed, (1, 0, 2, 3))
        packed = packed.reshape(clusters // 2, seq_devices * capacity, count * HD)
        return [packed[:, :, i * HD : (i + 1) * HD] for i in range(count)]

    def collect(arrays):
        count = len(arrays)
        joined = jnp.concatenate(arrays, axis=-1)
        joined = joined.reshape(clusters // 2, seq_devices, capacity, count * HD)
        joined = jnp.transpose(joined, (1, 0, 2, 3)).reshape(seq_devices, my_slots, count * HD)
        taken = jnp.einsum(
            "dst,dsf->dtf", one_hot, joined, preferred_element_type=jnp.float32
        ).astype(jnp.bfloat16)
        taken = taken.reshape(seq_devices, 2, half, count * HD)
        send = lax.dynamic_index_in_dim(taken, other, 1, keepdims=False)
        keep = lax.dynamic_index_in_dim(taken, core, 1, keepdims=False)
        summed = keep + swap_cores(send)
        landed = lax.all_to_all(summed, "seq", split_axis=0, concat_axis=0, tiled=True)
        landed = landed.reshape(2, heads, half, count * HD)
        theirs = swap_cores(pick(landed, other))
        rows = in_order(pick(landed, core), theirs, core, 0)
        rows = rows.reshape(2, heads, half, count, HD)
        rows = jnp.transpose(rows, (3, 0, 2, 1, 4)).reshape(count, tokens, features)
        return [rows[i] for i in range(count)]

    q_norm, q_factor = head_norm(queries[0])
    k_norm, k_factor = head_norm(key_rows[0])
    q_hat = q_norm.reshape(tokens, features).astype(jnp.bfloat16)
    k_hat = k_norm.reshape(tokens, features).astype(jnp.bfloat16)
    cotan = cotangent[0]
    w_full = lax.all_gather(w_out, "dp", axis=0, tiled=True)
    q_blk, k_blk, v_blk = dispatch([q_hat, k_hat, value_rows[0]])
    grad_attn = lax.dot_general(
        cotan, w_full, (((1,), (1,)), ((), ())), preferred_element_type=jnp.float32
    ).astype(jnp.bfloat16)
    (d_blk,) = dispatch([grad_attn])
    taken = jnp.sum(one_hot.astype(jnp.float32), axis=2)
    taken = taken.reshape(seq_devices, clusters // 2, capacity)
    key_valid = jnp.transpose(taken, (1, 0, 2)).reshape(clusters // 2, -1) > 0
    attn_blk, probs, probs_b = attend(q_blk, k_blk, v_blk, key_valid)
    (attn,) = collect([attn_blk])
    grads = attend_back(q_blk, k_blk, v_blk, probs, probs_b, attn_blk, d_blk)
    local_term = lax.dot_general(
        attn, cotan, (((0,), (0,)), ((), ())), preferred_element_type=jnp.float32
    )
    summed = lax.psum_scatter(local_term, ("seq", "dp"), scatter_dimension=0, tiled=True)
    weight_grad = summed / math.sqrt(tokens * seq_devices * 2)
    grad_qhat, grad_khat, grad_values = collect(list(grads))
    projected = jnp.dot(attn, w_full, preferred_element_type=jnp.float32).astype(jnp.bfloat16)
    grad_queries = norm_back(grad_qhat, q_norm, q_factor).astype(jnp.bfloat16)
    grad_keys = norm_back(grad_khat, k_norm, k_factor).astype(jnp.bfloat16)
    return (projected[None], grad_queries[None], grad_keys[None], grad_values[None], weight_grad)


def per_device(queries, *rest):
    heads = queries.shape[2] // HD
    if lax.axis_size("dp") == 2 and lax.axis_size("seq") == 2 * heads:
        return per_device_heads(queries, *rest)
    return per_device_slots(queries, *rest)


def solution(mesh):
    in_specs = (
        P("dp", "seq", None),
        P("dp", "seq", None),
        P("dp", "seq", None),
        P("dp", "seq", None),
        P("dp", None),
        P("dp", "seq"),
    )
    out_specs = (
        P("dp", "seq", None),
        P("dp", "seq", None),
        P("dp", "seq", None),
        P("dp", "seq", None),
        P(("seq", "dp"), None),
    )
    return jax.shard_map(
        per_device, mesh=mesh, in_specs=in_specs, out_specs=out_specs, check_vma=False
    )
```

```python
import functools
import math

import jax
import jax.numpy as jnp
from jax import lax
from jax.experimental import pallas as pl
from jax.experimental.pallas import tpu as pltpu
from jax.sharding import PartitionSpec as P

MESH = pl.DeviceIdType.MESH
HD = 128
CL_DEV = 4


EPS = 1e-06


def head_norm(matrix):
    shaped = matrix.astype(jnp.float32).reshape(matrix.shape[0], matrix.shape[1] // HD, HD)
    factor = lax.rsqrt(jnp.mean(shaped * shaped, axis=-1, keepdims=True) + EPS)
    return (shaped * factor, factor)


def norm_back(gradient, normed, factor):
    shaped = gradient.astype(jnp.float32).reshape(normed.shape)
    inner = jnp.mean(shaped * normed, axis=-1, keepdims=True)
    return (factor * (shaped - normed * inner)).reshape(normed.shape[0], -1)


def split_heads(blocks):
    return blocks.reshape(blocks.shape[0], blocks.shape[1], blocks.shape[2] // HD, HD)


def attend(q_blk, k_blk, v_blk, key_valid):
    q_four, k_four, v_four = (split_heads(q_blk), split_heads(k_blk), split_heads(v_blk))
    scores = jnp.einsum(
        "cqhd,ckhd->chqk", q_four, k_four, preferred_element_type=jnp.float32
    ) / math.sqrt(HD)
    positions = jnp.arange(q_blk.shape[1])
    below_diag = positions[None, :] <= positions[:, None]
    on_diagonal = positions[None, :] == positions[:, None]
    allowed = jnp.logical_or(
        jnp.logical_and(key_valid[:, None, None, :], below_diag[None, None]),
        on_diagonal[None, None],
    )
    weights = jnp.where(allowed, jnp.exp(scores), 0.0)
    probs = weights / jnp.sum(weights, axis=-1, keepdims=True)
    probs_b = probs.astype(jnp.bfloat16)
    attn = jnp.einsum(
        "chqk,ckhd->cqhd", probs_b, v_four, preferred_element_type=jnp.float32
    ).astype(jnp.bfloat16)
    return (attn.reshape(q_blk.shape), probs, probs_b)


def attend_back(q_blk, k_blk, v_blk, probs, probs_b, attn, d_blk):
    q_four, k_four, v_four = (split_heads(q_blk), split_heads(k_blk), split_heads(v_blk))
    d_four, a_four = (split_heads(d_blk), split_heads(attn))
    grad_value = jnp.einsum(
        "chqk,cqhd->ckhd", probs_b, d_four, preferred_element_type=jnp.float32
    ).astype(jnp.bfloat16)
    grad_prob = jnp.einsum("cqhd,ckhd->chqk", d_four, v_four, preferred_element_type=jnp.float32)
    delta_row = jnp.sum(d_four.astype(jnp.float32) * a_four.astype(jnp.float32), axis=-1)
    grad_score = (probs * (grad_prob - jnp.transpose(delta_row, (0, 2, 1))[..., None])).astype(
        jnp.bfloat16
    )
    grad_qhat = jnp.einsum(
        "chqk,ckhd->cqhd", grad_score, k_four, preferred_element_type=jnp.float32
    ) / math.sqrt(HD)
    grad_khat = jnp.einsum(
        "chqk,cqhd->ckhd", grad_score, q_four, preferred_element_type=jnp.float32
    ) / math.sqrt(HD)
    shape = q_blk.shape
    return (
        grad_qhat.astype(jnp.bfloat16).reshape(shape),
        grad_khat.astype(jnp.bfloat16).reshape(shape),
        grad_value.reshape(shape),
    )


def per_device_slots(queries, key_rows, value_rows, cotangent, w_out, cluster_ids):
    token_count = queries.shape[1]
    features = queries.shape[2]
    seq_devices = lax.axis_size("seq")
    data_devices = lax.axis_size("dp")
    capacity = 2 * token_count // (CL_DEV * seq_devices)
    total_slots = 2 * token_count
    labels = cluster_ids[0]
    positions = jnp.arange(token_count)
    matching = labels[:, None] == labels[None, :]
    earlier = positions[None, :] < positions[:, None]
    ranks = jnp.sum(jnp.logical_and(matching, earlier), axis=1)
    slot_index = labels * capacity + ranks

    def pack(matrix):
        empty = jnp.zeros((total_slots, matrix.shape[1]), matrix.dtype)
        return (
            empty.at[slot_index].set(matrix).reshape(seq_devices, CL_DEV, capacity, matrix.shape[1])
        )

    def unpack(returned):
        return returned.reshape(total_slots, -1)[slot_index]

    taken_slots = (
        jnp.zeros((total_slots,), jnp.bfloat16)
        .at[slot_index]
        .set(1.0)
        .reshape(seq_devices, CL_DEV, capacity)
    )
    q_norm, q_factor = head_norm(queries[0])
    k_norm, k_factor = head_norm(key_rows[0])
    q_hat = q_norm.reshape(token_count, features).astype(jnp.bfloat16)
    k_hat = k_norm.reshape(token_count, features).astype(jnp.bfloat16)
    cotan = cotangent[0]
    w_full = lax.all_gather(w_out, "dp", axis=0, tiled=True)
    received = (
        lax.all_to_all(pack(q_hat), "seq", split_axis=0, concat_axis=2, tiled=True),
        lax.all_to_all(pack(k_hat), "seq", split_axis=0, concat_axis=2, tiled=True),
        lax.all_to_all(pack(value_rows[0]), "seq", split_axis=0, concat_axis=2, tiled=True),
        lax.all_to_all(taken_slots, "seq", split_axis=0, concat_axis=2, tiled=True),
    )
    q_blk, k_blk, v_blk = (received[0][0], received[1][0], received[2][0])
    key_valid = received[3][0] > 0
    attn_blk, probs, probs_b = attend(q_blk, k_blk, v_blk, key_valid)
    attn_back = lax.all_to_all(attn_blk[None], "seq", split_axis=2, concat_axis=0, tiled=True)
    attn = unpack(attn_back)
    grad_attn = lax.dot_general(
        cotan, w_full, (((1,), (1,)), ((), ())), preferred_element_type=jnp.float32
    ).astype(jnp.bfloat16)
    grad_recv = lax.all_to_all(pack(grad_attn), "seq", split_axis=0, concat_axis=2, tiled=True)
    grad_qblk, grad_kblk, grad_vblk = attend_back(
        q_blk, k_blk, v_blk, probs, probs_b, attn_blk, grad_recv[0]
    )
    grads_back = (
        lax.all_to_all(grad_qblk[None], "seq", split_axis=2, concat_axis=0, tiled=True),
        lax.all_to_all(grad_kblk[None], "seq", split_axis=2, concat_axis=0, tiled=True),
        lax.all_to_all(grad_vblk[None], "seq", split_axis=2, concat_axis=0, tiled=True),
    )
    grad_qhat, grad_khat, grad_values = (
        unpack(grads_back[0]),
        unpack(grads_back[1]),
        unpack(grads_back[2]),
    )
    projected = jnp.dot(attn, w_full, preferred_element_type=jnp.float32).astype(jnp.bfloat16)
    grad_queries = norm_back(grad_qhat, q_norm, q_factor).astype(jnp.bfloat16)
    grad_keys = norm_back(grad_khat, k_norm, k_factor).astype(jnp.bfloat16)
    local_term = lax.dot_general(
        attn, cotan, (((0,), (0,)), ((), ())), preferred_element_type=jnp.float32
    )
    summed = lax.psum_scatter(local_term, ("seq", "dp"), scatter_dimension=0, tiled=True)
    weight_grad = summed / math.sqrt(token_count * seq_devices * data_devices)
    return (projected[None], grad_queries[None], grad_keys[None], grad_values[None], weight_grad)


def greet_all(seq_devices):
    barrier = pltpu.get_barrier_semaphore()
    me = lax.axis_index("seq") * 2 + lax.axis_index("dp")
    everyone = 2 * seq_devices

    def greet(step, carry):
        peer = lax.rem(me + step, everyone)
        pl.semaphore_signal(
            barrier, inc=1, device_id=(peer // 2, lax.rem(peer, 2)), device_id_type=MESH
        )
        return carry

    lax.fori_loop(1, everyone, greet, 0)
    pl.semaphore_wait(barrier, everyone - 1)


def remote(source, target, sent, landed, device):
    return pltpu.make_async_remote_copy(
        src_ref=source,
        dst_ref=target,
        send_sem=sent,
        recv_sem=landed,
        device_id=device,
        device_id_type=MESH,
    )


def dispatch_kernel(
    heads, x_ref, ids_ref, full_ref, slots_ref, sent, landed, relay_sent, relay_landed, id_sent, id_landed
):
    seq_devices = 2 * heads
    chip, core = lax.axis_index("seq"), lax.axis_index("dp")
    other = 1 - core
    seq_here, head_here = chip // heads, lax.rem(chip, heads)
    greet_all(seq_devices)

    def target(step):
        part = lax.rem(step, 2)
        head = lax.rem(chip + step // 2, heads)
        return part, head, core * heads + head

    def data_copy(step):
        part, head, owner = target(step)
        return remote(
            x_ref.at[head, part],
            full_ref.at[chip, part],
            sent.at[step],
            landed.at[chip],
            (owner, part),
        )

    def id_copy(step):
        part, head, owner = target(step)
        return remote(
            ids_ref, slots_ref.at[chip], id_sent.at[step], id_landed.at[chip], (owner, part)
        )

    def to_self(step):
        part, head, owner = target(step)
        return jnp.logical_and(owner == chip, part == core)

    def send(step, carry):
        part, head, owner = target(step)

        @pl.when(jnp.logical_not(to_self(step)))
        def _():
            id_copy(step).start()
            data_copy(step).start()

        @pl.when(to_self(step))
        def _():
            full_ref[chip, part] = x_ref[head, part]
            slots_ref[chip] = ids_ref[...]

        return carry

    lax.fori_loop(0, seq_devices, send, 0)

    def relay_copy(source):
        return remote(
            full_ref.at[source, core],
            full_ref.at[source, core],
            relay_sent.at[source],
            relay_landed.at[source],
            (chip, other),
        )

    def receive(step, carry):
        source = lax.rem(head_here - step // 2 + heads, heads) + heads * lax.rem(step, 2)

        @pl.when(jnp.logical_not(jnp.logical_and(source == chip, seq_here == core)))
        def _():
            remote(
                x_ref.at[0, 0],
                full_ref.at[source, core],
                sent.at[0],
                landed.at[source],
                (chip, other),
            ).wait_recv()
            remote(
                ids_ref, slots_ref.at[source], id_sent.at[0], id_landed.at[source], (chip, other)
            ).wait_recv()

        relay_copy(source).start()
        return carry

    lax.fori_loop(0, seq_devices, receive, 0)

    def finish(step, carry):
        remote(
            full_ref.at[step, core],
            full_ref.at[step, other],
            relay_sent.at[step],
            relay_landed.at[step],
            (chip, other),
        ).wait_recv()
        relay_copy(step).wait_send()

        @pl.when(jnp.logical_not(to_self(step)))
        def _():
            id_copy(step).wait_send()
            data_copy(step).wait_send()

        return carry

    lax.fori_loop(0, seq_devices, finish, 0)


def dispatch_call(x, ids):
    heads, _, half, width = x.shape
    n = 2 * heads
    vmem = pl.BlockSpec(memory_space=pltpu.VMEM)
    return pl.pallas_call(
        functools.partial(dispatch_kernel, heads),
        out_shape=(
            jax.ShapeDtypeStruct((n, 2, half, width), x.dtype),
            jax.ShapeDtypeStruct((n,) + ids.shape, ids.dtype),
        ),
        in_specs=[vmem, vmem],
        out_specs=(vmem, vmem),
        scratch_shapes=[pltpu.SemaphoreType.DMA((n,))] * 6,
        compiler_params=pltpu.CompilerParams(
            collective_id=0, has_side_effects=True, vmem_limit_bytes=40 << 20
        ),
        cost_estimate=pl.CostEstimate(flops=0, bytes_accessed=x.size * 6, transcendentals=0),
    )(x, ids)


def collect_kernel(heads, scale, *refs):
    seq_devices = 2 * heads
    if scale is None:
        t_ref, out_ref, held, stage, swap_sent, swap_landed, sent, landed = refs
        w_ref = None
    else:
        (
            t_ref, w_ref, out_ref, grad_ref, held, stage, swap_sent, swap_landed, sent, landed,
            w_held, w_stage, w_parts, w_swap_sent, w_swap_landed, w_sent, w_landed,
        ) = refs
    chip, core = lax.axis_index("seq"), lax.axis_index("dp")
    other = 1 - core
    seq_here, head_here = chip // heads, lax.rem(chip, heads)
    greet_all(seq_devices)

    def peer_of(step):
        return lax.rem(chip + step, seq_devices)

    def swap(peer):
        return remote(
            t_ref.at[other, peer],
            held.at[peer],
            swap_sent.at[peer],
            swap_landed.at[peer],
            (chip, other),
        )

    def w_swap(peer):
        return remote(
            w_ref.at[peer, other],
            w_held.at[peer],
            w_swap_sent.at[peer],
            w_swap_landed.at[peer],
            (chip, other),
        )

    def begin(step, carry):
        if w_ref is not None:
            w_swap(peer_of(step)).start()
        swap(peer_of(step)).start()
        return carry

    lax.fori_loop(0, seq_devices, begin, 0)

    def send_copy(peer):
        return remote(
            stage.at[peer],
            out_ref.at[head_here, core],
            sent.at[peer],
            landed.at[2 * head_here + core],
            (peer, seq_here),
        )

    def w_copy(peer):
        return remote(
            w_stage.at[peer], w_parts.at[chip], w_sent.at[peer], w_landed.at[chip], (peer, core)
        )

    def to_self(peer):
        return jnp.logical_and(peer == chip, seq_here == core)

    def send(step, carry):
        peer = peer_of(step)
        if w_ref is not None:
            w_swap(peer).wait_recv()
            total = w_ref[peer, core].astype(jnp.float32) + w_held[peer].astype(jnp.float32)

            @pl.when(peer != chip)
            def _():
                w_stage[peer] = total.astype(w_stage.dtype)
                w_copy(peer).start()

            @pl.when(peer == chip)
            def _():
                w_parts[chip] = total.astype(w_parts.dtype)

        swap(peer).wait_recv()

        @pl.when(jnp.logical_not(to_self(peer)))
        def _():
            stage[peer] = t_ref[core, peer] + held[peer]
            send_copy(peer).start()

        @pl.when(to_self(peer))
        def _():
            out_ref[head_here, core] = t_ref[core, peer] + held[peer]

        return carry

    lax.fori_loop(0, seq_devices, send, 0)

    if w_ref is not None:
        grad_ref[...] = jnp.zeros_like(grad_ref)

        def add(step, carry):
            source = lax.rem(chip - step + seq_devices, seq_devices)

            @pl.when(source != chip)
            def _():
                remote(
                    w_stage.at[source],
                    w_parts.at[source],
                    w_sent.at[source],
                    w_landed.at[source],
                    (source, core),
                ).wait_recv()

            grad_ref[...] += w_parts[source].astype(jnp.float32)
            return carry

        lax.fori_loop(0, seq_devices, add, 0)
        grad_ref[...] = grad_ref[...] * scale

    def finish(step, carry):
        head, part = step // 2, lax.rem(step, 2)
        source = core * heads + head

        @pl.when(jnp.logical_not(jnp.logical_and(source == chip, part == core)))
        def _():
            remote(
                stage.at[0], out_ref.at[head, part], sent.at[0], landed.at[step], (chip, other)
            ).wait_recv()

        swap(step).wait_send()

        @pl.when(jnp.logical_not(to_self(step)))
        def _():
            send_copy(step).wait_send()

        if w_ref is not None:
            w_swap(step).wait_send()

            @pl.when(step != chip)
            def _():
                w_copy(step).wait_send()

        return carry

    lax.fori_loop(0, seq_devices, finish, 0)


def collect_call(heads, rows, terms=None, scale=None):
    _, n, half, width = rows.shape
    vmem = pl.BlockSpec(memory_space=pltpu.VMEM)
    out_shape = [jax.ShapeDtypeStruct((heads, 2, half, width), rows.dtype)]
    block = (n, half, width)
    scratch = [pltpu.VMEM(block, rows.dtype)] * 2 + [pltpu.SemaphoreType.DMA((n,))] * 4
    args = [rows]
    if terms is not None:
        args.append(terms)
        w_block = (n,) + terms.shape[2:]
        out_shape.append(jax.ShapeDtypeStruct(terms.shape[2:], jnp.float32))
        scratch += [pltpu.VMEM(w_block, terms.dtype)] * 3 + [pltpu.SemaphoreType.DMA((n,))] * 4
    return pl.pallas_call(
        functools.partial(collect_kernel, heads, scale),
        out_shape=tuple(out_shape),
        in_specs=[vmem] * len(args),
        out_specs=(vmem,) * len(out_shape),
        scratch_shapes=scratch,
        compiler_params=pltpu.CompilerParams(
            collective_id=1 if terms is None else 2,
            has_side_effects=True,
            vmem_limit_bytes=40 << 20,
        ),
        cost_estimate=pl.CostEstimate(flops=0, bytes_accessed=rows.size * 6, transcendentals=0),
    )(*args)


def per_device_heads(queries, key_rows, value_rows, cotangent, w_out, cluster_ids):
    tokens, features = queries.shape[1], queries.shape[2]
    heads = features // HD
    seq_devices = lax.axis_size("seq")
    half = tokens // 2
    clusters = CL_DEV * seq_devices
    capacity = 2 * tokens // clusters
    core = lax.axis_index("dp")
    labels = cluster_ids[0]
    positions = jnp.arange(tokens)
    matching = labels[:, None] == labels[None, :]
    earlier = positions[None, :] < positions[:, None]
    ranks = jnp.sum(jnp.logical_and(matching, earlier), axis=1)
    slot_index = (labels * capacity + ranks).astype(jnp.int32)
    ids = jnp.broadcast_to(slot_index[None, :], (8, tokens))

    q_norm, q_factor = head_norm(queries[0])
    k_norm, k_factor = head_norm(key_rows[0])
    q_hat = q_norm.reshape(tokens, features).astype(jnp.bfloat16)
    k_hat = k_norm.reshape(tokens, features).astype(jnp.bfloat16)
    cotan = cotangent[0]
    w_full = lax.all_gather(w_out, "dp", axis=0, tiled=True)
    grad_attn = lax.dot_general(
        cotan, w_full, (((1,), (1,)), ((), ())), preferred_element_type=jnp.float32
    ).astype(jnp.bfloat16)
    arrays = [q_hat, k_hat, value_rows[0], grad_attn]
    width = len(arrays) * HD
    stacked = jnp.concatenate(
        [a.reshape(2, half, heads, HD).transpose(2, 0, 1, 3) for a in arrays], axis=-1
    )
    full, landed_ids = dispatch_call(stacked, ids)
    slots = landed_ids[:, 0, :]
    my_slots = clusters * capacity // 2
    wanted = core * my_slots + jnp.arange(my_slots)
    one_hot = (slots[:, None, :] == wanted[None, :, None]).astype(jnp.bfloat16)
    packed = jnp.einsum(
        "dst,dtf->dsf",
        one_hot,
        full.reshape(seq_devices, tokens, width),
        preferred_element_type=jnp.float32,
    ).astype(jnp.bfloat16)
    packed = packed.reshape(seq_devices, clusters // 2, capacity, width)
    packed = jnp.transpose(packed, (1, 0, 2, 3))
    packed = packed.reshape(clusters // 2, seq_devices * capacity, width)
    q_blk, k_blk, v_blk, d_blk = [packed[:, :, i * HD : (i + 1) * HD] for i in range(4)]
    taken = jnp.sum(one_hot.astype(jnp.float32), axis=2)
    taken = taken.reshape(seq_devices, clusters // 2, capacity)
    key_valid = jnp.transpose(taken, (1, 0, 2)).reshape(clusters // 2, -1) > 0

    def take(blocks):
        count = len(blocks)
        joined = jnp.concatenate(blocks, axis=-1)
        joined = joined.reshape(clusters // 2, seq_devices, capacity, count * HD)
        joined = jnp.transpose(joined, (1, 0, 2, 3)).reshape(seq_devices, my_slots, count * HD)
        rows = jnp.einsum(
            "dspt,dsf->pdtf",
            one_hot.reshape(seq_devices, my_slots, 2, half),
            joined,
            preferred_element_type=jnp.float32,
        )
        return rows.astype(jnp.bfloat16)

    def whole_rows(out, index):
        rows = out[:, :, :, index * HD : (index + 1) * HD]
        return jnp.transpose(rows, (1, 2, 0, 3)).reshape(tokens, features)

    attn_blk, probs, probs_b = attend(q_blk, k_blk, v_blk, key_valid)
    (attn_out,) = collect_call(heads, take([attn_blk]))
    attn = whole_rows(attn_out, 0)
    grads = attend_back(q_blk, k_blk, v_blk, probs, probs_b, attn_blk, d_blk)
    local_term = lax.dot_general(
        attn, cotan, (((0,), (0,)), ((), ())), preferred_element_type=jnp.float32
    ).astype(jnp.bfloat16)
    local_term = local_term.reshape(seq_devices, 2, features // (2 * seq_devices), -1)
    scale = 1.0 / math.sqrt(tokens * seq_devices * 2)
    grads_out, weight_grad = collect_call(heads, take(list(grads)), local_term, scale)
    grad_qhat, grad_khat, grad_values = [whole_rows(grads_out, i) for i in range(3)]
    projected = jnp.dot(attn, w_full, preferred_element_type=jnp.float32).astype(jnp.bfloat16)
    grad_queries = norm_back(grad_qhat, q_norm, q_factor).astype(jnp.bfloat16)
    grad_keys = norm_back(grad_khat, k_norm, k_factor).astype(jnp.bfloat16)
    return (projected[None], grad_queries[None], grad_keys[None], grad_values[None], weight_grad)


def per_device(queries, *rest):
    heads = queries.shape[2] // HD
    if lax.axis_size("dp") == 2 and lax.axis_size("seq") == 2 * heads:
        return per_device_heads(queries, *rest)
    return per_device_slots(queries, *rest)


def solution(mesh):
    in_specs = (
        P("dp", "seq", None),
        P("dp", "seq", None),
        P("dp", "seq", None),
        P("dp", "seq", None),
        P("dp", None),
        P("dp", "seq"),
    )
    out_specs = (
        P("dp", "seq", None),
        P("dp", "seq", None),
        P("dp", "seq", None),
        P("dp", "seq", None),
        P(("seq", "dp"), None),
    )
    return jax.shard_map(
        per_device, mesh=mesh, in_specs=in_specs, out_specs=out_specs, check_vma=False
    )
```

```python
import functools
import math

import jax
import jax.numpy as jnp
from jax import lax
from jax.experimental import pallas as pl
from jax.experimental.pallas import tpu as pltpu
from jax.sharding import PartitionSpec as P

MESH = pl.DeviceIdType.MESH
HD = 128
CL_DEV = 4


EPS = 1e-06


def head_norm(matrix):
    shaped = matrix.astype(jnp.float32).reshape(matrix.shape[0], matrix.shape[1] // HD, HD)
    factor = lax.rsqrt(jnp.mean(shaped * shaped, axis=-1, keepdims=True) + EPS)
    return (shaped * factor, factor)


def norm_back(gradient, normed, factor):
    shaped = gradient.astype(jnp.float32).reshape(normed.shape)
    inner = jnp.mean(shaped * normed, axis=-1, keepdims=True)
    return (factor * (shaped - normed * inner)).reshape(normed.shape[0], -1)


def split_heads(blocks):
    return blocks.reshape(blocks.shape[0], blocks.shape[1], blocks.shape[2] // HD, HD)


def attend(q_blk, k_blk, v_blk, key_valid):
    q_four, k_four, v_four = (split_heads(q_blk), split_heads(k_blk), split_heads(v_blk))
    scores = jnp.einsum(
        "cqhd,ckhd->chqk", q_four, k_four, preferred_element_type=jnp.float32
    ) / math.sqrt(HD)
    positions = jnp.arange(q_blk.shape[1])
    below_diag = positions[None, :] <= positions[:, None]
    on_diagonal = positions[None, :] == positions[:, None]
    allowed = jnp.logical_or(
        jnp.logical_and(key_valid[:, None, None, :], below_diag[None, None]),
        on_diagonal[None, None],
    )
    weights = jnp.where(allowed, jnp.exp(scores), 0.0)
    probs = weights / jnp.sum(weights, axis=-1, keepdims=True)
    probs_b = probs.astype(jnp.bfloat16)
    attn = jnp.einsum(
        "chqk,ckhd->cqhd", probs_b, v_four, preferred_element_type=jnp.float32
    ).astype(jnp.bfloat16)
    return (attn.reshape(q_blk.shape), probs, probs_b)


def attend_back(q_blk, k_blk, v_blk, probs, probs_b, attn, d_blk):
    q_four, k_four, v_four = (split_heads(q_blk), split_heads(k_blk), split_heads(v_blk))
    d_four, a_four = (split_heads(d_blk), split_heads(attn))
    grad_value = jnp.einsum(
        "chqk,cqhd->ckhd", probs_b, d_four, preferred_element_type=jnp.float32
    ).astype(jnp.bfloat16)
    grad_prob = jnp.einsum("cqhd,ckhd->chqk", d_four, v_four, preferred_element_type=jnp.float32)
    delta_row = jnp.sum(d_four.astype(jnp.float32) * a_four.astype(jnp.float32), axis=-1)
    grad_score = (probs * (grad_prob - jnp.transpose(delta_row, (0, 2, 1))[..., None])).astype(
        jnp.bfloat16
    )
    grad_qhat = jnp.einsum(
        "chqk,ckhd->cqhd", grad_score, k_four, preferred_element_type=jnp.float32
    ) / math.sqrt(HD)
    grad_khat = jnp.einsum(
        "chqk,cqhd->ckhd", grad_score, q_four, preferred_element_type=jnp.float32
    ) / math.sqrt(HD)
    shape = q_blk.shape
    return (
        grad_qhat.astype(jnp.bfloat16).reshape(shape),
        grad_khat.astype(jnp.bfloat16).reshape(shape),
        grad_value.reshape(shape),
    )


def per_device_slots(queries, key_rows, value_rows, cotangent, w_out, cluster_ids):
    token_count = queries.shape[1]
    features = queries.shape[2]
    seq_devices = lax.axis_size("seq")
    data_devices = lax.axis_size("dp")
    capacity = 2 * token_count // (CL_DEV * seq_devices)
    total_slots = 2 * token_count
    labels = cluster_ids[0]
    positions = jnp.arange(token_count)
    matching = labels[:, None] == labels[None, :]
    earlier = positions[None, :] < positions[:, None]
    ranks = jnp.sum(jnp.logical_and(matching, earlier), axis=1)
    slot_index = labels * capacity + ranks

    def pack(matrix):
        empty = jnp.zeros((total_slots, matrix.shape[1]), matrix.dtype)
        return (
            empty.at[slot_index].set(matrix).reshape(seq_devices, CL_DEV, capacity, matrix.shape[1])
        )

    def unpack(returned):
        return returned.reshape(total_slots, -1)[slot_index]

    taken_slots = (
        jnp.zeros((total_slots,), jnp.bfloat16)
        .at[slot_index]
        .set(1.0)
        .reshape(seq_devices, CL_DEV, capacity)
    )
    q_norm, q_factor = head_norm(queries[0])
    k_norm, k_factor = head_norm(key_rows[0])
    q_hat = q_norm.reshape(token_count, features).astype(jnp.bfloat16)
    k_hat = k_norm.reshape(token_count, features).astype(jnp.bfloat16)
    cotan = cotangent[0]
    w_full = lax.all_gather(w_out, "dp", axis=0, tiled=True)
    received = (
        lax.all_to_all(pack(q_hat), "seq", split_axis=0, concat_axis=2, tiled=True),
        lax.all_to_all(pack(k_hat), "seq", split_axis=0, concat_axis=2, tiled=True),
        lax.all_to_all(pack(value_rows[0]), "seq", split_axis=0, concat_axis=2, tiled=True),
        lax.all_to_all(taken_slots, "seq", split_axis=0, concat_axis=2, tiled=True),
    )
    q_blk, k_blk, v_blk = (received[0][0], received[1][0], received[2][0])
    key_valid = received[3][0] > 0
    attn_blk, probs, probs_b = attend(q_blk, k_blk, v_blk, key_valid)
    attn_back = lax.all_to_all(attn_blk[None], "seq", split_axis=2, concat_axis=0, tiled=True)
    attn = unpack(attn_back)
    grad_attn = lax.dot_general(
        cotan, w_full, (((1,), (1,)), ((), ())), preferred_element_type=jnp.float32
    ).astype(jnp.bfloat16)
    grad_recv = lax.all_to_all(pack(grad_attn), "seq", split_axis=0, concat_axis=2, tiled=True)
    grad_qblk, grad_kblk, grad_vblk = attend_back(
        q_blk, k_blk, v_blk, probs, probs_b, attn_blk, grad_recv[0]
    )
    grads_back = (
        lax.all_to_all(grad_qblk[None], "seq", split_axis=2, concat_axis=0, tiled=True),
        lax.all_to_all(grad_kblk[None], "seq", split_axis=2, concat_axis=0, tiled=True),
        lax.all_to_all(grad_vblk[None], "seq", split_axis=2, concat_axis=0, tiled=True),
    )
    grad_qhat, grad_khat, grad_values = (
        unpack(grads_back[0]),
        unpack(grads_back[1]),
        unpack(grads_back[2]),
    )
    projected = jnp.dot(attn, w_full, preferred_element_type=jnp.float32).astype(jnp.bfloat16)
    grad_queries = norm_back(grad_qhat, q_norm, q_factor).astype(jnp.bfloat16)
    grad_keys = norm_back(grad_khat, k_norm, k_factor).astype(jnp.bfloat16)
    local_term = lax.dot_general(
        attn, cotan, (((0,), (0,)), ((), ())), preferred_element_type=jnp.float32
    )
    summed = lax.psum_scatter(local_term, ("seq", "dp"), scatter_dimension=0, tiled=True)
    weight_grad = summed / math.sqrt(token_count * seq_devices * data_devices)
    return (projected[None], grad_queries[None], grad_keys[None], grad_values[None], weight_grad)


def greet_all(seq_devices):
    barrier = pltpu.get_barrier_semaphore()
    me = lax.axis_index("seq") * 2 + lax.axis_index("dp")
    everyone = 2 * seq_devices

    def greet(step, carry):
        peer = lax.rem(me + step, everyone)
        pl.semaphore_signal(
            barrier, inc=1, device_id=(peer // 2, lax.rem(peer, 2)), device_id_type=MESH
        )
        return carry

    lax.fori_loop(1, everyone, greet, 0)
    pl.semaphore_wait(barrier, everyone - 1)


def remote(source, target, sent, landed, device):
    return pltpu.make_async_remote_copy(
        src_ref=source,
        dst_ref=target,
        send_sem=sent,
        recv_sem=landed,
        device_id=device,
        device_id_type=MESH,
    )


def normalize(rows):
    wide = rows.astype(jnp.float32)
    factor = lax.rsqrt(jnp.mean(wide * wide, axis=-1, keepdims=True) + EPS)
    return wide * factor, factor


def lanes(head):
    return pl.ds(pl.multiple_of(head * HD, HD), HD)


def dispatch_kernel(
    heads, q_ref, k_ref, v_ref, c_ref, w_ref, ids_ref, full_ref, slots_ref, w_full_ref, x_ref,
    sent, landed, relay_sent, relay_landed, id_sent, id_landed, w_sent, w_landed,
):
    seq_devices = 2 * heads
    chip, core = lax.axis_index("seq"), lax.axis_index("dp")
    other = 1 - core
    seq_here, head_here = chip // heads, lax.rem(chip, heads)
    half = x_ref.shape[2]
    per_core = heads // 2
    greet_all(seq_devices)
    w_copy = remote(w_ref, w_full_ref.at[core], w_sent, w_landed, (chip, other))
    w_copy.start()
    w_full_ref[core] = w_ref[...]

    def target(step):
        part = lax.rem(step, 2)
        head = lax.rem(chip + step // 2, heads)
        return part, head, core * heads + head

    def data_copy(step):
        part, head, owner = target(step)
        return remote(
            x_ref.at[head, part],
            full_ref.at[chip, part],
            sent.at[step],
            landed.at[chip],
            (owner, part),
        )

    def id_copy(step):
        part, head, owner = target(step)
        return remote(
            ids_ref, slots_ref.at[chip], id_sent.at[step], id_landed.at[chip], (owner, part)
        )

    def to_self(step):
        part, head, owner = target(step)
        return jnp.logical_and(owner == chip, part == core)

    def send(step):
        part, head, owner = target(step)

        @pl.when(jnp.logical_not(to_self(step)))
        def _():
            id_copy(step).start()
            data_copy(step).start()

        @pl.when(to_self(step))
        def _():
            full_ref[chip, part] = x_ref[head, part]
            slots_ref[chip] = ids_ref[...]

    def fill(head, index, rows):
        for part in range(2):
            x_ref[head, part, :, index * HD : (index + 1) * HD] = rows[
                part * half : (part + 1) * half
            ].astype(x_ref.dtype)

    remote(w_ref, w_full_ref.at[other], w_sent, w_landed, (chip, other)).wait_recv()

    def prepare(step, carry):
        head = lax.rem(chip + step, heads)
        fill(head, 0, normalize(q_ref[:, lanes(head)])[0])
        fill(head, 1, normalize(k_ref[:, lanes(head)])[0])
        fill(head, 2, v_ref[:, lanes(head)])
        w_rows = w_full_ref[head // per_core, lanes(lax.rem(head, per_core)), :]
        grad = lax.dot_general(
            c_ref[...], w_rows, (((1,), (1,)), ((), ())), preferred_element_type=jnp.float32
        )
        fill(head, 3, grad)
        send(2 * step)
        send(2 * step + 1)
        return carry

    lax.fori_loop(0, heads, prepare, 0)

    def relay_copy(source):
        return remote(
            full_ref.at[source, core],
            full_ref.at[source, core],
            relay_sent.at[source],
            relay_landed.at[source],
            (chip, other),
        )

    def receive(step, carry):
        source = lax.rem(head_here - step // 2 + heads, heads) + heads * lax.rem(step, 2)

        @pl.when(jnp.logical_not(jnp.logical_and(source == chip, seq_here == core)))
        def _():
            remote(
                x_ref.at[0, 0],
                full_ref.at[source, core],
                sent.at[0],
                landed.at[source],
                (chip, other),
            ).wait_recv()
            remote(
                ids_ref, slots_ref.at[source], id_sent.at[0], id_landed.at[source], (chip, other)
            ).wait_recv()

        relay_copy(source).start()
        return carry

    lax.fori_loop(0, seq_devices, receive, 0)

    def finish(step, carry):
        remote(
            full_ref.at[step, core],
            full_ref.at[step, other],
            relay_sent.at[step],
            relay_landed.at[step],
            (chip, other),
        ).wait_recv()
        relay_copy(step).wait_send()

        @pl.when(jnp.logical_not(to_self(step)))
        def _():
            id_copy(step).wait_send()
            data_copy(step).wait_send()

        return carry

    lax.fori_loop(0, seq_devices, finish, 0)
    w_copy.wait_send()


def dispatch_call(q, k, v, c, w, ids):
    tokens, features = q.shape
    heads = features // HD
    half, width = tokens // 2, 4 * HD
    n = 2 * heads
    vmem = pl.BlockSpec(memory_space=pltpu.VMEM)
    return pl.pallas_call(
        functools.partial(dispatch_kernel, heads),
        out_shape=(
            jax.ShapeDtypeStruct((n, 2, half, width), q.dtype),
            jax.ShapeDtypeStruct((n,) + ids.shape, ids.dtype),
            jax.ShapeDtypeStruct((2,) + w.shape, w.dtype),
        ),
        in_specs=[vmem] * 6,
        out_specs=(vmem,) * 3,
        scratch_shapes=[pltpu.VMEM((heads, 2, half, width), q.dtype)]
        + [pltpu.SemaphoreType.DMA((n,))] * 6
        + [pltpu.SemaphoreType.DMA] * 2,
        compiler_params=pltpu.CompilerParams(
            collective_id=0, has_side_effects=True, vmem_limit_bytes=40 << 20
        ),
    )(q, k, v, c, w, ids)


def collect_kernel(heads, t_ref, out_ref, held, stage, swap_sent, swap_landed, sent, landed):
    start_swaps, send_all, wait_one = collector(
        heads, t_ref, out_ref, held, stage, swap_sent, swap_landed, sent, landed
    )
    greet_all(2 * heads)
    start_swaps()
    send_all()
    lax.fori_loop(0, 2 * heads, lambda step, carry: wait_one(step, carry), 0)


def collector(heads, t_ref, out_ref, held, stage, swap_sent, swap_landed, sent, landed):
    seq_devices = 2 * heads
    chip, core = lax.axis_index("seq"), lax.axis_index("dp")
    other = 1 - core
    seq_here, head_here = chip // heads, lax.rem(chip, heads)

    def peer_of(step):
        return lax.rem(chip + step, seq_devices)

    def swap(peer):
        return remote(
            t_ref.at[other, peer],
            held.at[peer],
            swap_sent.at[peer],
            swap_landed.at[peer],
            (chip, other),
        )

    def send_copy(peer):
        return remote(
            stage.at[peer],
            out_ref.at[head_here, core],
            sent.at[peer],
            landed.at[2 * head_here + core],
            (peer, seq_here),
        )

    def to_self(peer):
        return jnp.logical_and(peer == chip, seq_here == core)

    def begin(step, carry):
        swap(peer_of(step)).start()
        return carry

    def send(step, carry):
        peer = peer_of(step)
        swap(peer).wait_recv()

        @pl.when(jnp.logical_not(to_self(peer)))
        def _():
            stage[peer] = t_ref[core, peer] + held[peer]
            send_copy(peer).start()

        @pl.when(to_self(peer))
        def _():
            out_ref[head_here, core] = t_ref[core, peer] + held[peer]

        return carry

    def wait_one(step, carry):
        head, part = step // 2, lax.rem(step, 2)
        source = core * heads + head

        @pl.when(jnp.logical_not(jnp.logical_and(source == chip, part == core)))
        def _():
            remote(
                stage.at[0], out_ref.at[head, part], sent.at[0], landed.at[step], (chip, other)
            ).wait_recv()

        swap(step).wait_send()

        @pl.when(jnp.logical_not(to_self(step)))
        def _():
            send_copy(step).wait_send()

        return carry

    return (
        lambda: lax.fori_loop(0, seq_devices, begin, 0),
        lambda: lax.fori_loop(0, seq_devices, send, 0),
        wait_one,
    )


def final_kernel(
    heads, scale, t_ref, w_ref, q_ref, k_ref, a_ref, proj_ref,
    gq_ref, gk_ref, gv_ref, out_ref, grad_ref,
    got, held, stage, w_held, kept, x_stage, x_got, y_stage, y_got, z_stage, z_got,
    swap_sent, swap_landed, sent, landed, w_swap_sent, w_swap_landed,
    x_sent, x_landed, y_sent, y_landed, z_sent, z_landed,
):
    seq_devices = 2 * heads
    quarter = seq_devices // 4
    chip, core = lax.axis_index("seq"), lax.axis_index("dp")
    other = 1 - core
    x, y, z = lax.rem(chip, 2), lax.rem(chip // 2, 2), chip // 4
    half = got.shape[2]
    start_swaps, send_all, wait_one = collector(
        heads, t_ref, got, held, stage, swap_sent, swap_landed, sent, landed
    )
    greet_all(seq_devices)

    def w_swap(peer):
        return remote(
            w_ref.at[peer, other],
            w_held.at[peer],
            w_swap_sent.at[peer],
            w_swap_landed.at[peer],
            (chip, other),
        )

    def x_copy(j):
        return remote(
            x_stage.at[j], x_got.at[j], x_sent.at[j], x_landed.at[j], (chip + 1 - 2 * x, core)
        )

    def y_copy(j):
        return remote(
            y_stage.at[j], y_got.at[j], y_sent.at[j], y_landed.at[j], (chip + 2 - 4 * y, core)
        )

    def z_copy(j):
        return remote(
            z_stage.at[j], z_got.at[z], z_sent.at[j], z_landed.at[z], (4 * j + 2 * y + x, core)
        )

    def both_cores(peer):
        w_swap(peer).wait_recv()
        return w_ref[peer, core].astype(jnp.float32) + w_held[peer].astype(jnp.float32)

    def begin(step, carry):
        w_swap(step).start()
        return carry

    def x_phase(j, carry):
        x_stage[j] = both_cores(2 * j + 1 - x).astype(x_stage.dtype)
        x_copy(j).start()
        kept[j] = both_cores(2 * j + x)
        return carry

    def y_phase(j, carry):
        away, here = 2 * j + 1 - y, 2 * j + y
        x_copy(away).wait_recv()
        y_stage[j] = (kept[away] + x_got[away].astype(jnp.float32)).astype(y_stage.dtype)
        y_copy(j).start()
        x_copy(here).wait_recv()
        kept[here] += x_got[here].astype(jnp.float32)
        return carry

    def z_phase(j, carry):
        y_copy(j).wait_recv()
        total = kept[2 * j + y] + y_got[j].astype(jnp.float32)

        @pl.when(j != z)
        def _():
            z_stage[j] = total.astype(z_stage.dtype)
            z_copy(j).start()

        @pl.when(j == z)
        def _():
            grad_ref[...] = total

        return carry

    def z_sum(j, carry):
        @pl.when(j != z)
        def _():
            remote(
                z_stage.at[j], z_got.at[j], z_sent.at[j], z_landed.at[j], (4 * j + 2 * y + x, core)
            ).wait_recv()
            grad_ref[...] += z_got[j].astype(jnp.float32)
            z_copy(j).wait_send()

        y_copy(j).wait_send()
        return carry

    def ends(j, carry):
        x_copy(j).wait_send()
        w_swap(2 * j).wait_send()
        w_swap(2 * j + 1).wait_send()
        return carry

    lax.fori_loop(0, seq_devices, begin, 0)
    start_swaps()
    lax.fori_loop(0, seq_devices // 2, x_phase, 0)
    send_all()
    lax.fori_loop(0, quarter, y_phase, 0)
    lax.fori_loop(0, quarter, z_phase, 0)

    depth = proj_ref.shape[1]
    tile = 2 * HD

    def project(step, carry):
        columns = pl.ds(pl.multiple_of(step * tile, tile), tile)
        total = jnp.dot(
            a_ref[:, :depth], proj_ref[0, :, columns], preferred_element_type=jnp.float32
        ) + jnp.dot(a_ref[:, depth:], proj_ref[1, :, columns], preferred_element_type=jnp.float32)
        out_ref[:, columns] = total.astype(out_ref.dtype)
        return carry

    lax.fori_loop(0, out_ref.shape[1] // tile, project, 0)

    def finish(step, carry):
        wait_one(step, carry)
        head, part = step // 2, lax.rem(step, 2)
        rows = pl.ds(pl.multiple_of(part * half, half), half)
        for index, (source, target) in enumerate(((q_ref, gq_ref), (k_ref, gk_ref))):
            normed, factor = normalize(source[rows, lanes(head)])
            gradient = got[head, part, :, index * HD : (index + 1) * HD].astype(jnp.float32)
            inner = jnp.mean(gradient * normed, axis=-1, keepdims=True)
            target[rows, lanes(head)] = (factor * (gradient - normed * inner)).astype(target.dtype)
        gv_ref[rows, lanes(head)] = got[head, part, :, 2 * HD :]
        return carry

    lax.fori_loop(0, seq_devices, finish, 0)
    lax.fori_loop(0, quarter, z_sum, 0)
    grad_ref[...] = grad_ref[...] * scale
    lax.fori_loop(0, seq_devices // 2, ends, 0)


def final_call(heads, scale, rows, terms, q, k, attn, w_full):
    _, n, half, width = rows.shape
    vmem = pl.BlockSpec(memory_space=pltpu.VMEM)
    piece = terms.shape[2:]
    kind = rows.dtype
    args = (rows, terms, q, k, attn, w_full)
    like = jax.ShapeDtypeStruct(q.shape, kind)
    projected = jax.ShapeDtypeStruct((q.shape[0], w_full.shape[2]), kind)
    counts = [n] * 6 + [n // 2] * 2 + [n // 4] * 4
    return pl.pallas_call(
        functools.partial(final_kernel, heads, scale),
        out_shape=(like, like, like, projected, jax.ShapeDtypeStruct(piece, jnp.float32)),
        in_specs=[vmem] * len(args),
        out_specs=(vmem,) * 5,
        scratch_shapes=[
            pltpu.VMEM((heads, 2, half, width), kind),
            pltpu.VMEM((n, half, width), kind),
            pltpu.VMEM((n, half, width), kind),
            pltpu.VMEM((n,) + piece, kind),
            pltpu.VMEM((n // 2,) + piece, jnp.float32),
            pltpu.VMEM((n // 2,) + piece, kind),
            pltpu.VMEM((n // 2,) + piece, kind),
        ]
        + [pltpu.VMEM((n // 4,) + piece, kind)] * 4
        + [pltpu.SemaphoreType.DMA((count,)) for count in counts],
        compiler_params=pltpu.CompilerParams(
            collective_id=2, has_side_effects=True, vmem_limit_bytes=48 << 20
        ),
    )(*args)


def collect_call(heads, rows):
    _, n, half, width = rows.shape
    vmem = pl.BlockSpec(memory_space=pltpu.VMEM)
    return pl.pallas_call(
        functools.partial(collect_kernel, heads),
        out_shape=jax.ShapeDtypeStruct((heads, 2, half, width), rows.dtype),
        in_specs=[vmem],
        out_specs=vmem,
        scratch_shapes=[pltpu.VMEM((n, half, width), rows.dtype)] * 2
        + [pltpu.SemaphoreType.DMA((n,))] * 4,
        compiler_params=pltpu.CompilerParams(
            collective_id=1, has_side_effects=True, vmem_limit_bytes=40 << 20
        ),
    )(rows)


def per_device_heads(queries, key_rows, value_rows, cotangent, w_out, cluster_ids):
    tokens, features = queries.shape[1], queries.shape[2]
    heads = features // HD
    seq_devices = lax.axis_size("seq")
    half = tokens // 2
    clusters = CL_DEV * seq_devices
    capacity = 2 * tokens // clusters
    core = lax.axis_index("dp")
    labels = cluster_ids[0]
    positions = jnp.arange(tokens)
    matching = labels[:, None] == labels[None, :]
    earlier = positions[None, :] < positions[:, None]
    ranks = jnp.sum(jnp.logical_and(matching, earlier), axis=1)
    slot_index = (labels * capacity + ranks).astype(jnp.int32)
    ids = jnp.broadcast_to(slot_index[None, :], (8, tokens))

    cotan = cotangent[0]
    width = 4 * HD
    full, landed_ids, w_full = dispatch_call(
        queries[0], key_rows[0], value_rows[0], cotan, w_out, ids
    )
    slots = landed_ids[:, 0, :]
    my_slots = clusters * capacity // 2
    wanted = core * my_slots + jnp.arange(my_slots)
    one_hot = (slots[:, None, :] == wanted[None, :, None]).astype(jnp.bfloat16)
    packed = jnp.einsum(
        "dst,dtf->dsf",
        one_hot,
        full.reshape(seq_devices, tokens, width),
        preferred_element_type=jnp.float32,
    ).astype(jnp.bfloat16)
    packed = packed.reshape(seq_devices, clusters // 2, capacity, width)
    packed = jnp.transpose(packed, (1, 0, 2, 3))
    packed = packed.reshape(clusters // 2, seq_devices * capacity, width)
    q_blk, k_blk, v_blk, d_blk = [packed[:, :, i * HD : (i + 1) * HD] for i in range(4)]
    taken = jnp.sum(one_hot.astype(jnp.float32), axis=2)
    taken = taken.reshape(seq_devices, clusters // 2, capacity)
    key_valid = jnp.transpose(taken, (1, 0, 2)).reshape(clusters // 2, -1) > 0

    def take(blocks):
        count = len(blocks)
        joined = jnp.concatenate(blocks, axis=-1)
        joined = joined.reshape(clusters // 2, seq_devices, capacity, count * HD)
        joined = jnp.transpose(joined, (1, 0, 2, 3)).reshape(seq_devices, my_slots, count * HD)
        rows = jnp.einsum(
            "dspt,dsf->pdtf",
            one_hot.reshape(seq_devices, my_slots, 2, half),
            joined,
            preferred_element_type=jnp.float32,
        )
        return rows.astype(jnp.bfloat16)

    def whole_rows(out, index):
        rows = out[:, :, :, index * HD : (index + 1) * HD]
        return jnp.transpose(rows, (1, 2, 0, 3)).reshape(tokens, features)

    attn_blk, probs, probs_b = attend(q_blk, k_blk, v_blk, key_valid)
    attn_out = collect_call(heads, take([attn_blk]))
    attn = whole_rows(attn_out, 0)
    grads = attend_back(q_blk, k_blk, v_blk, probs, probs_b, attn_blk, d_blk)
    local_term = lax.dot_general(
        attn, cotan, (((0,), (0,)), ((), ())), preferred_element_type=jnp.float32
    ).astype(jnp.bfloat16)
    local_term = local_term.reshape(seq_devices, 2, features // (2 * seq_devices), -1)
    scale = 1.0 / math.sqrt(tokens * seq_devices * 2)
    grad_queries, grad_keys, grad_values, projected, weight_grad = final_call(
        heads, scale, take(list(grads)), local_term, queries[0], key_rows[0], attn, w_full
    )
    return (projected[None], grad_queries[None], grad_keys[None], grad_values[None], weight_grad)


def per_device(queries, *rest):
    heads = queries.shape[2] // HD
    if lax.axis_size("dp") == 2 and lax.axis_size("seq") == 2 * heads:
        return per_device_heads(queries, *rest)
    return per_device_slots(queries, *rest)


def solution(mesh):
    in_specs = (
        P("dp", "seq", None),
        P("dp", "seq", None),
        P("dp", "seq", None),
        P("dp", "seq", None),
        P("dp", None),
        P("dp", "seq"),
    )
    out_specs = (
        P("dp", "seq", None),
        P("dp", "seq", None),
        P("dp", "seq", None),
        P("dp", "seq", None),
        P(("seq", "dp"), None),
    )
    return jax.shard_map(
        per_device, mesh=mesh, in_specs=in_specs, out_specs=out_specs, check_vma=False
    )
```

```python
import functools
import math

import jax
import jax.numpy as jnp
from jax import lax
from jax.experimental import pallas as pl
from jax.experimental.pallas import tpu as pltpu
from jax.sharding import PartitionSpec as P

MESH = pl.DeviceIdType.MESH
HD = 128
CL_DEV = 4


EPS = 1e-06


def head_norm(matrix):
    shaped = matrix.astype(jnp.float32).reshape(matrix.shape[0], matrix.shape[1] // HD, HD)
    factor = lax.rsqrt(jnp.mean(shaped * shaped, axis=-1, keepdims=True) + EPS)
    return (shaped * factor, factor)


def norm_back(gradient, normed, factor):
    shaped = gradient.astype(jnp.float32).reshape(normed.shape)
    inner = jnp.mean(shaped * normed, axis=-1, keepdims=True)
    return (factor * (shaped - normed * inner)).reshape(normed.shape[0], -1)


def split_heads(blocks):
    return blocks.reshape(blocks.shape[0], blocks.shape[1], blocks.shape[2] // HD, HD)


def attend(q_blk, k_blk, v_blk, key_valid):
    q_four, k_four, v_four = (split_heads(q_blk), split_heads(k_blk), split_heads(v_blk))
    scores = jnp.einsum(
        "cqhd,ckhd->chqk", q_four, k_four, preferred_element_type=jnp.float32
    ) / math.sqrt(HD)
    positions = jnp.arange(q_blk.shape[1])
    below_diag = positions[None, :] <= positions[:, None]
    on_diagonal = positions[None, :] == positions[:, None]
    allowed = jnp.logical_or(
        jnp.logical_and(key_valid[:, None, None, :], below_diag[None, None]),
        on_diagonal[None, None],
    )
    weights = jnp.where(allowed, jnp.exp(scores), 0.0)
    probs = weights / jnp.sum(weights, axis=-1, keepdims=True)
    probs_b = probs.astype(jnp.bfloat16)
    attn = jnp.einsum(
        "chqk,ckhd->cqhd", probs_b, v_four, preferred_element_type=jnp.float32
    ).astype(jnp.bfloat16)
    return (attn.reshape(q_blk.shape), probs, probs_b)


def attend_back(q_blk, k_blk, v_blk, probs, probs_b, attn, d_blk):
    q_four, k_four, v_four = (split_heads(q_blk), split_heads(k_blk), split_heads(v_blk))
    d_four, a_four = (split_heads(d_blk), split_heads(attn))
    grad_value = jnp.einsum(
        "chqk,cqhd->ckhd", probs_b, d_four, preferred_element_type=jnp.float32
    ).astype(jnp.bfloat16)
    grad_prob = jnp.einsum("cqhd,ckhd->chqk", d_four, v_four, preferred_element_type=jnp.float32)
    delta_row = jnp.sum(d_four.astype(jnp.float32) * a_four.astype(jnp.float32), axis=-1)
    grad_score = (probs * (grad_prob - jnp.transpose(delta_row, (0, 2, 1))[..., None])).astype(
        jnp.bfloat16
    )
    grad_qhat = jnp.einsum(
        "chqk,ckhd->cqhd", grad_score, k_four, preferred_element_type=jnp.float32
    ) / math.sqrt(HD)
    grad_khat = jnp.einsum(
        "chqk,cqhd->ckhd", grad_score, q_four, preferred_element_type=jnp.float32
    ) / math.sqrt(HD)
    shape = q_blk.shape
    return (
        grad_qhat.astype(jnp.bfloat16).reshape(shape),
        grad_khat.astype(jnp.bfloat16).reshape(shape),
        grad_value.reshape(shape),
    )


def per_device_slots(queries, key_rows, value_rows, cotangent, w_out, cluster_ids):
    token_count = queries.shape[1]
    features = queries.shape[2]
    seq_devices = lax.axis_size("seq")
    data_devices = lax.axis_size("dp")
    capacity = 2 * token_count // (CL_DEV * seq_devices)
    total_slots = 2 * token_count
    labels = cluster_ids[0]
    positions = jnp.arange(token_count)
    matching = labels[:, None] == labels[None, :]
    earlier = positions[None, :] < positions[:, None]
    ranks = jnp.sum(jnp.logical_and(matching, earlier), axis=1)
    slot_index = labels * capacity + ranks

    def pack(matrix):
        empty = jnp.zeros((total_slots, matrix.shape[1]), matrix.dtype)
        return (
            empty.at[slot_index].set(matrix).reshape(seq_devices, CL_DEV, capacity, matrix.shape[1])
        )

    def unpack(returned):
        return returned.reshape(total_slots, -1)[slot_index]

    taken_slots = (
        jnp.zeros((total_slots,), jnp.bfloat16)
        .at[slot_index]
        .set(1.0)
        .reshape(seq_devices, CL_DEV, capacity)
    )
    q_norm, q_factor = head_norm(queries[0])
    k_norm, k_factor = head_norm(key_rows[0])
    q_hat = q_norm.reshape(token_count, features).astype(jnp.bfloat16)
    k_hat = k_norm.reshape(token_count, features).astype(jnp.bfloat16)
    cotan = cotangent[0]
    w_full = lax.all_gather(w_out, "dp", axis=0, tiled=True)
    received = (
        lax.all_to_all(pack(q_hat), "seq", split_axis=0, concat_axis=2, tiled=True),
        lax.all_to_all(pack(k_hat), "seq", split_axis=0, concat_axis=2, tiled=True),
        lax.all_to_all(pack(value_rows[0]), "seq", split_axis=0, concat_axis=2, tiled=True),
        lax.all_to_all(taken_slots, "seq", split_axis=0, concat_axis=2, tiled=True),
    )
    q_blk, k_blk, v_blk = (received[0][0], received[1][0], received[2][0])
    key_valid = received[3][0] > 0
    attn_blk, probs, probs_b = attend(q_blk, k_blk, v_blk, key_valid)
    attn_back = lax.all_to_all(attn_blk[None], "seq", split_axis=2, concat_axis=0, tiled=True)
    attn = unpack(attn_back)
    grad_attn = lax.dot_general(
        cotan, w_full, (((1,), (1,)), ((), ())), preferred_element_type=jnp.float32
    ).astype(jnp.bfloat16)
    grad_recv = lax.all_to_all(pack(grad_attn), "seq", split_axis=0, concat_axis=2, tiled=True)
    grad_qblk, grad_kblk, grad_vblk = attend_back(
        q_blk, k_blk, v_blk, probs, probs_b, attn_blk, grad_recv[0]
    )
    grads_back = (
        lax.all_to_all(grad_qblk[None], "seq", split_axis=2, concat_axis=0, tiled=True),
        lax.all_to_all(grad_kblk[None], "seq", split_axis=2, concat_axis=0, tiled=True),
        lax.all_to_all(grad_vblk[None], "seq", split_axis=2, concat_axis=0, tiled=True),
    )
    grad_qhat, grad_khat, grad_values = (
        unpack(grads_back[0]),
        unpack(grads_back[1]),
        unpack(grads_back[2]),
    )
    projected = jnp.dot(attn, w_full, preferred_element_type=jnp.float32).astype(jnp.bfloat16)
    grad_queries = norm_back(grad_qhat, q_norm, q_factor).astype(jnp.bfloat16)
    grad_keys = norm_back(grad_khat, k_norm, k_factor).astype(jnp.bfloat16)
    local_term = lax.dot_general(
        attn, cotan, (((0,), (0,)), ((), ())), preferred_element_type=jnp.float32
    )
    summed = lax.psum_scatter(local_term, ("seq", "dp"), scatter_dimension=0, tiled=True)
    weight_grad = summed / math.sqrt(token_count * seq_devices * data_devices)
    return (projected[None], grad_queries[None], grad_keys[None], grad_values[None], weight_grad)


def greet_all(seq_devices):
    barrier = pltpu.get_barrier_semaphore()
    me = lax.axis_index("seq") * 2 + lax.axis_index("dp")
    everyone = 2 * seq_devices

    def greet(step, carry):
        peer = lax.rem(me + step, everyone)
        pl.semaphore_signal(
            barrier, inc=1, device_id=(peer // 2, lax.rem(peer, 2)), device_id_type=MESH
        )
        return carry

    lax.fori_loop(1, everyone, greet, 0)
    pl.semaphore_wait(barrier, everyone - 1)


def remote(source, target, sent, landed, device):
    return pltpu.make_async_remote_copy(
        src_ref=source,
        dst_ref=target,
        send_sem=sent,
        recv_sem=landed,
        device_id=device,
        device_id_type=MESH,
    )


def normalize(rows):
    wide = rows.astype(jnp.float32)
    factor = lax.rsqrt(jnp.mean(wide * wide, axis=-1, keepdims=True) + EPS)
    return wide * factor, factor


def lanes(head):
    return pl.ds(pl.multiple_of(head * HD, HD), HD)


def dispatch_kernel(
    heads, q_in, k_in, v_in, c_in, w_ref, ids_ref, full_ref, slots_ref, w_full_ref, x_ref,
    q_ref, k_ref, v_ref, c_ref, loaded, sent, landed, relay_sent, relay_landed, id_sent, id_landed, w_sent, w_landed,
):
    seq_devices = 2 * heads
    chip, core = lax.axis_index("seq"), lax.axis_index("dp")
    other = 1 - core
    seq_here, head_here = chip // heads, lax.rem(chip, heads)
    half = x_ref.shape[2]
    per_core = heads // 2
    pairs = ((q_in, q_ref), (k_in, k_ref), (v_in, v_ref), (c_in, c_ref), (w_ref, w_full_ref.at[core]))
    loads = [
        pltpu.make_async_copy(source, target, loaded.at[i])
        for i, (source, target) in enumerate(pairs)
    ]
    for load in loads:
        load.start()
    greet_all(seq_devices)
    w_copy = remote(w_ref, w_full_ref.at[core], w_sent, w_landed, (chip, other))
    w_copy.start()
    for load in loads:
        load.wait()

    def target(step):
        part = lax.rem(step, 2)
        head = lax.rem(chip + step // 2, heads)
        return part, head, core * heads + head

    def data_copy(step):
        part, head, owner = target(step)
        return remote(
            x_ref.at[head, part],
            full_ref.at[chip, part],
            sent.at[step],
            landed.at[chip],
            (owner, part),
        )

    def id_copy(step):
        part, head, owner = target(step)
        return remote(
            ids_ref, slots_ref.at[chip], id_sent.at[step], id_landed.at[chip], (owner, part)
        )

    def to_self(step):
        part, head, owner = target(step)
        return jnp.logical_and(owner == chip, part == core)

    def send(step):
        part, head, owner = target(step)

        @pl.when(jnp.logical_not(to_self(step)))
        def _():
            id_copy(step).start()
            data_copy(step).start()

        @pl.when(to_self(step))
        def _():
            full_ref[chip, part] = x_ref[head, part]
            slots_ref[chip] = ids_ref[...]

    def fill(head, index, rows):
        for part in range(2):
            x_ref[head, part, :, index * HD : (index + 1) * HD] = rows[
                part * half : (part + 1) * half
            ].astype(x_ref.dtype)

    def prepare(step, carry):
        head = lax.rem(chip + step, heads)
        fill(head, 0, normalize(q_ref[:, lanes(head)])[0])
        fill(head, 1, normalize(k_ref[:, lanes(head)])[0])
        fill(head, 2, v_ref[:, lanes(head)])

        @pl.when(step == 0)
        def _():
            remote(w_ref, w_full_ref.at[other], w_sent, w_landed, (chip, other)).wait_recv()

        w_rows = w_full_ref[head // per_core, lanes(lax.rem(head, per_core)), :]
        grad = lax.dot_general(
            c_ref[...], w_rows, (((1,), (1,)), ((), ())), preferred_element_type=jnp.float32
        )
        fill(head, 3, grad)
        send(2 * step)
        send(2 * step + 1)
        return carry

    lax.fori_loop(0, heads, prepare, 0)

    def relay_copy(source):
        return remote(
            full_ref.at[source, core],
            full_ref.at[source, core],
            relay_sent.at[source],
            relay_landed.at[source],
            (chip, other),
        )

    def receive(step, carry):
        source = lax.rem(head_here - step // 2 + heads, heads) + heads * lax.rem(step, 2)

        @pl.when(jnp.logical_not(jnp.logical_and(source == chip, seq_here == core)))
        def _():
            remote(
                x_ref.at[0, 0],
                full_ref.at[source, core],
                sent.at[0],
                landed.at[source],
                (chip, other),
            ).wait_recv()
            remote(
                ids_ref, slots_ref.at[source], id_sent.at[0], id_landed.at[source], (chip, other)
            ).wait_recv()

        relay_copy(source).start()
        return carry

    lax.fori_loop(0, seq_devices, receive, 0)

    def finish(step, carry):
        remote(
            full_ref.at[step, core],
            full_ref.at[step, other],
            relay_sent.at[step],
            relay_landed.at[step],
            (chip, other),
        ).wait_recv()
        relay_copy(step).wait_send()

        @pl.when(jnp.logical_not(to_self(step)))
        def _():
            id_copy(step).wait_send()
            data_copy(step).wait_send()

        return carry

    lax.fori_loop(0, seq_devices, finish, 0)
    w_copy.wait_send()


def dispatch_call(q, k, v, c, w, ids):
    tokens, features = q.shape
    heads = features // HD
    half, width = tokens // 2, 4 * HD
    n = 2 * heads
    vmem = pl.BlockSpec(memory_space=pltpu.VMEM)
    return pl.pallas_call(
        functools.partial(dispatch_kernel, heads),
        out_shape=(
            jax.ShapeDtypeStruct((n, 2, half, width), q.dtype),
            jax.ShapeDtypeStruct((n,) + ids.shape, ids.dtype),
            jax.ShapeDtypeStruct((2,) + w.shape, w.dtype),
        ),
        in_specs=[pl.BlockSpec(memory_space=pl.ANY)] * 5 + [vmem],
        out_specs=(vmem,) * 3,
        scratch_shapes=[pltpu.VMEM((heads, 2, half, width), q.dtype)]
        + [pltpu.VMEM(q.shape, q.dtype)] * 3
        + [pltpu.VMEM(c.shape, c.dtype), pltpu.SemaphoreType.DMA((5,))]
        + [pltpu.SemaphoreType.DMA((n,))] * 6
        + [pltpu.SemaphoreType.DMA] * 2,
        compiler_params=pltpu.CompilerParams(
            collective_id=0, has_side_effects=True, vmem_limit_bytes=40 << 20
        ),
    )(q, k, v, c, w, ids)


def collector(heads, t_ref, out_ref, held, stage, swap_sent, swap_landed, sent, landed):
    seq_devices = 2 * heads
    chip, core = lax.axis_index("seq"), lax.axis_index("dp")
    other = 1 - core
    seq_here, head_here = chip // heads, lax.rem(chip, heads)

    def peer_of(step):
        far = heads * (1 - lax.rem(step, 2))
        return lax.rem(chip + step // 2 + far, seq_devices)

    def swap(peer):
        return remote(
            t_ref.at[other, peer],
            held.at[peer],
            swap_sent.at[peer],
            swap_landed.at[peer],
            (chip, other),
        )

    def send_copy(peer):
        return remote(
            stage.at[peer],
            out_ref.at[head_here, core],
            sent.at[peer],
            landed.at[2 * head_here + core],
            (peer, seq_here),
        )

    def to_self(peer):
        return jnp.logical_and(peer == chip, seq_here == core)

    def begin(step, carry):
        swap(peer_of(step)).start()
        return carry

    def send(step, carry):
        peer = peer_of(step)
        swap(peer).wait_recv()

        @pl.when(jnp.logical_not(to_self(peer)))
        def _():
            stage[peer] = t_ref[core, peer] + held[peer]
            send_copy(peer).start()

        @pl.when(to_self(peer))
        def _():
            out_ref[head_here, core] = t_ref[core, peer] + held[peer]

        return carry

    def wait_one(step, carry):
        head, part = step // 2, lax.rem(step, 2)
        source = core * heads + head

        @pl.when(jnp.logical_not(jnp.logical_and(source == chip, part == core)))
        def _():
            remote(
                stage.at[0], out_ref.at[head, part], sent.at[0], landed.at[step], (chip, other)
            ).wait_recv()

        swap(step).wait_send()

        @pl.when(jnp.logical_not(to_self(step)))
        def _():
            send_copy(step).wait_send()

        return carry

    return (
        lambda: lax.fori_loop(0, seq_devices, begin, 0),
        lambda low, high: lax.fori_loop(low, high, send, 0),
        wait_one,
    )


def final_kernel(
    heads, scale, t_ref, t_attn, q_ref, k_ref, c_ref, proj_ref,
    gq_ref, gk_ref, gv_ref, out_ref, grad_ref,
    got, held, stage, got_attn, held_attn, stage_attn, a_ref, w_ref, w_held, kept, x_stage, x_got, y_stage, y_got, z_stage, z_got,
    swap_sent, swap_landed, sent, landed, w_swap_sent, w_swap_landed,
    attn_swap_sent, attn_swap_landed, attn_sent, attn_landed,
    x_sent, x_landed, y_sent, y_landed, z_sent, z_landed,
):
    seq_devices = 2 * heads
    quarter = seq_devices // 4
    chip, core = lax.axis_index("seq"), lax.axis_index("dp")
    other = 1 - core
    x, y, z = lax.rem(chip, 2), lax.rem(chip // 2, 2), chip // 4
    half = got.shape[2]
    start_swaps, send_all, wait_one = collector(
        heads, t_ref, got, held, stage, swap_sent, swap_landed, sent, landed
    )
    start_attn, send_attn, wait_attn = collector(
        heads, t_attn, got_attn, held_attn, stage_attn,
        attn_swap_sent, attn_swap_landed, attn_sent, attn_landed,
    )
    greet_all(seq_devices)

    def w_swap(peer):
        return remote(
            w_ref.at[peer, other],
            w_held.at[peer],
            w_swap_sent.at[peer],
            w_swap_landed.at[peer],
            (chip, other),
        )

    def x_copy(j):
        return remote(
            x_stage.at[j], x_got.at[j], x_sent.at[j], x_landed.at[j], (chip + 1 - 2 * x, core)
        )

    def y_copy(j):
        return remote(
            y_stage.at[j], y_got.at[j], y_sent.at[j], y_landed.at[j], (chip + 2 - 4 * y, core)
        )

    def z_copy(j):
        return remote(
            z_stage.at[j], z_got.at[z], z_sent.at[j], z_landed.at[z], (4 * j + 2 * y + x, core)
        )

    def both_cores(peer):
        w_swap(peer).wait_recv()
        return w_ref[peer, core].astype(jnp.float32) + w_held[peer].astype(jnp.float32)

    piece = w_ref.shape[2]

    def term(head, carry):
        total = None
        for part in range(2):
            wait_attn(2 * head + part, 0)
            rows = slice(part * half, (part + 1) * half)
            block = got_attn[head, part]
            a_ref[rows, lanes(head)] = block
            partial = lax.dot_general(
                block, c_ref[rows, :], (((0,), (0,)), ((), ())), preferred_element_type=jnp.float32
            )
            total = partial if total is None else total + partial
        for index in range(4):
            w_ref[2 * head + index // 2, index % 2] = total[
                index * piece : (index + 1) * piece
            ].astype(w_ref.dtype)
        w_swap(2 * head).start()
        w_swap(2 * head + 1).start()
        return carry

    def x_phase(j, carry):
        x_stage[j] = both_cores(2 * j + 1 - x).astype(x_stage.dtype)
        x_copy(j).start()
        kept[j] = both_cores(2 * j + x)
        return carry

    def y_phase(j, carry):
        away, here = 2 * j + 1 - y, 2 * j + y
        x_copy(away).wait_recv()
        y_stage[j] = (kept[away] + x_got[away].astype(jnp.float32)).astype(y_stage.dtype)
        y_copy(j).start()
        x_copy(here).wait_recv()
        kept[here] += x_got[here].astype(jnp.float32)
        return carry

    def z_phase(j, carry):
        y_copy(j).wait_recv()
        total = kept[2 * j + y] + y_got[j].astype(jnp.float32)

        @pl.when(j != z)
        def _():
            z_stage[j] = total.astype(z_stage.dtype)
            z_copy(j).start()

        @pl.when(j == z)
        def _():
            grad_ref[...] = total

        return carry

    def z_sum(j, carry):
        @pl.when(j != z)
        def _():
            remote(
                z_stage.at[j], z_got.at[j], z_sent.at[j], z_landed.at[j], (4 * j + 2 * y + x, core)
            ).wait_recv()
            grad_ref[...] += z_got[j].astype(jnp.float32)
            z_copy(j).wait_send()

        y_copy(j).wait_send()
        return carry

    def ends(j, carry):
        x_copy(j).wait_send()
        w_swap(2 * j).wait_send()
        w_swap(2 * j + 1).wait_send()
        return carry

    start_attn()
    start_swaps()
    send_attn(0, seq_devices)
    send_all(0, heads)
    lax.fori_loop(0, heads, term, 0)
    lax.fori_loop(0, seq_devices // 2, x_phase, 0)
    send_all(heads, seq_devices)
    lax.fori_loop(0, quarter, y_phase, 0)
    lax.fori_loop(0, quarter, z_phase, 0)

    depth = proj_ref.shape[1]
    tile = 2 * HD

    def project(step, carry):
        columns = pl.ds(pl.multiple_of(step * tile, tile), tile)
        total = jnp.dot(
            a_ref[:, :depth], proj_ref[0, :, columns], preferred_element_type=jnp.float32
        ) + jnp.dot(a_ref[:, depth:], proj_ref[1, :, columns], preferred_element_type=jnp.float32)
        out_ref[:, columns] = total.astype(out_ref.dtype)
        return carry

    lax.fori_loop(0, out_ref.shape[1] // tile, project, 0)

    def finish(step, carry):
        wait_one(step, carry)
        head, part = step // 2, lax.rem(step, 2)
        rows = pl.ds(pl.multiple_of(part * half, half), half)
        for index, (source, target) in enumerate(((q_ref, gq_ref), (k_ref, gk_ref))):
            normed, factor = normalize(source[rows, lanes(head)])
            gradient = got[head, part, :, index * HD : (index + 1) * HD].astype(jnp.float32)
            inner = jnp.mean(gradient * normed, axis=-1, keepdims=True)
            target[rows, lanes(head)] = (factor * (gradient - normed * inner)).astype(target.dtype)
        gv_ref[rows, lanes(head)] = got[head, part, :, 2 * HD :]
        return carry

    lax.fori_loop(0, seq_devices, finish, 0)
    lax.fori_loop(0, quarter, z_sum, 0)
    grad_ref[...] = grad_ref[...] * scale
    lax.fori_loop(0, seq_devices // 2, ends, 0)


def final_call(heads, scale, rows, attn_rows, q, k, cotan, w_full):
    _, n, half, width = rows.shape
    vmem = pl.BlockSpec(memory_space=pltpu.VMEM)
    piece = (q.shape[1] // (2 * n), w_full.shape[2])
    kind = rows.dtype
    args = (rows, attn_rows, q, k, cotan, w_full)
    like = jax.ShapeDtypeStruct(q.shape, kind)
    projected = jax.ShapeDtypeStruct((q.shape[0], w_full.shape[2]), kind)
    counts = [n] * 10 + [n // 2] * 2 + [n // 4] * 4
    return pl.pallas_call(
        functools.partial(final_kernel, heads, scale),
        out_shape=(like, like, like, projected, jax.ShapeDtypeStruct(piece, jnp.float32)),
        in_specs=[vmem] * len(args),
        out_specs=(vmem,) * 5,
        scratch_shapes=[
            pltpu.VMEM((heads, 2, half, width), kind),
            pltpu.VMEM((n, half, width), kind),
            pltpu.VMEM((n, half, width), kind),
            pltpu.VMEM((heads, 2, half, HD), kind),
            pltpu.VMEM((n, half, HD), kind),
            pltpu.VMEM((n, half, HD), kind),
            pltpu.VMEM(q.shape, kind),
            pltpu.VMEM((n, 2) + piece, kind),
            pltpu.VMEM((n,) + piece, kind),
            pltpu.VMEM((n // 2,) + piece, jnp.float32),
            pltpu.VMEM((n // 2,) + piece, kind),
            pltpu.VMEM((n // 2,) + piece, kind),
        ]
        + [pltpu.VMEM((n // 4,) + piece, kind)] * 4
        + [pltpu.SemaphoreType.DMA((count,)) for count in counts],
        compiler_params=pltpu.CompilerParams(
            collective_id=2, has_side_effects=True, vmem_limit_bytes=48 << 20
        ),
    )(*args)


def per_device_heads(queries, key_rows, value_rows, cotangent, w_out, cluster_ids):
    tokens, features = queries.shape[1], queries.shape[2]
    heads = features // HD
    seq_devices = lax.axis_size("seq")
    half = tokens // 2
    clusters = CL_DEV * seq_devices
    capacity = 2 * tokens // clusters
    core = lax.axis_index("dp")
    labels = cluster_ids[0]
    positions = jnp.arange(tokens)
    matching = labels[:, None] == labels[None, :]
    earlier = positions[None, :] < positions[:, None]
    ranks = jnp.sum(jnp.logical_and(matching, earlier), axis=1)
    slot_index = (labels * capacity + ranks).astype(jnp.int32)
    ids = jnp.broadcast_to(slot_index[None, :], (8, tokens))

    cotan = cotangent[0]
    width = 4 * HD
    full, landed_ids, w_full = dispatch_call(
        queries[0], key_rows[0], value_rows[0], cotan, w_out, ids
    )
    slots = landed_ids[:, 0, :]
    my_slots = clusters * capacity // 2
    wanted = core * my_slots + jnp.arange(my_slots)
    one_hot = (slots[:, None, :] == wanted[None, :, None]).astype(jnp.bfloat16)
    packed = jnp.einsum(
        "dst,dtf->dsf",
        one_hot,
        full.reshape(seq_devices, tokens, width),
        preferred_element_type=jnp.float32,
    ).astype(jnp.bfloat16)
    packed = packed.reshape(seq_devices, clusters // 2, capacity, width)
    packed = jnp.transpose(packed, (1, 0, 2, 3))
    packed = packed.reshape(clusters // 2, seq_devices * capacity, width)
    q_blk, k_blk, v_blk, d_blk = [packed[:, :, i * HD : (i + 1) * HD] for i in range(4)]
    taken = jnp.sum(one_hot.astype(jnp.float32), axis=2)
    taken = taken.reshape(seq_devices, clusters // 2, capacity)
    key_valid = jnp.transpose(taken, (1, 0, 2)).reshape(clusters // 2, -1) > 0

    def take(blocks):
        count = len(blocks)
        joined = jnp.concatenate(blocks, axis=-1)
        joined = joined.reshape(clusters // 2, seq_devices, capacity, count * HD)
        joined = jnp.transpose(joined, (1, 0, 2, 3)).reshape(seq_devices, my_slots, count * HD)
        rows = jnp.einsum(
            "dspt,dsf->pdtf",
            one_hot.reshape(seq_devices, my_slots, 2, half),
            joined,
            preferred_element_type=jnp.float32,
        )
        return rows.astype(jnp.bfloat16)

    attn_blk, probs, probs_b = attend(q_blk, k_blk, v_blk, key_valid)
    grads = attend_back(q_blk, k_blk, v_blk, probs, probs_b, attn_blk, d_blk)
    scale = 1.0 / math.sqrt(tokens * seq_devices * 2)
    grad_queries, grad_keys, grad_values, projected, weight_grad = final_call(
        heads, scale, take(list(grads)), take([attn_blk]), queries[0], key_rows[0], cotan, w_full
    )
    return (projected[None], grad_queries[None], grad_keys[None], grad_values[None], weight_grad)


def per_device(queries, *rest):
    heads = queries.shape[2] // HD
    if lax.axis_size("dp") == 2 and lax.axis_size("seq") == 2 * heads:
        return per_device_heads(queries, *rest)
    return per_device_slots(queries, *rest)


def solution(mesh):
    in_specs = (
        P("dp", "seq", None),
        P("dp", "seq", None),
        P("dp", "seq", None),
        P("dp", "seq", None),
        P("dp", None),
        P("dp", "seq"),
    )
    out_specs = (
        P("dp", "seq", None),
        P("dp", "seq", None),
        P("dp", "seq", None),
        P("dp", "seq", None),
        P(("seq", "dp"), None),
    )
    return jax.shard_map(
        per_device, mesh=mesh, in_specs=in_specs, out_specs=out_specs, check_vma=False
    )
```

```python
import functools
import math

import jax
import jax.numpy as jnp
from jax import lax
from jax.experimental import pallas as pl
from jax.experimental.pallas import tpu as pltpu
from jax.sharding import PartitionSpec as P

MESH = pl.DeviceIdType.MESH
HD = 128
CL_DEV = 4


EPS = 1e-06


def head_norm(matrix):
    shaped = matrix.astype(jnp.float32).reshape(matrix.shape[0], matrix.shape[1] // HD, HD)
    factor = lax.rsqrt(jnp.mean(shaped * shaped, axis=-1, keepdims=True) + EPS)
    return (shaped * factor, factor)


def norm_back(gradient, normed, factor):
    shaped = gradient.astype(jnp.float32).reshape(normed.shape)
    inner = jnp.mean(shaped * normed, axis=-1, keepdims=True)
    return (factor * (shaped - normed * inner)).reshape(normed.shape[0], -1)


def split_heads(blocks):
    return blocks.reshape(blocks.shape[0], blocks.shape[1], blocks.shape[2] // HD, HD)


def attend(q_blk, k_blk, v_blk, key_valid):
    q_four, k_four, v_four = (split_heads(q_blk), split_heads(k_blk), split_heads(v_blk))
    scores = jnp.einsum(
        "cqhd,ckhd->chqk", q_four, k_four, preferred_element_type=jnp.float32
    ) / math.sqrt(HD)
    positions = jnp.arange(q_blk.shape[1])
    below_diag = positions[None, :] <= positions[:, None]
    on_diagonal = positions[None, :] == positions[:, None]
    allowed = jnp.logical_or(
        jnp.logical_and(key_valid[:, None, None, :], below_diag[None, None]),
        on_diagonal[None, None],
    )
    weights = jnp.where(allowed, jnp.exp(scores), 0.0)
    probs = weights / jnp.sum(weights, axis=-1, keepdims=True)
    probs_b = probs.astype(jnp.bfloat16)
    attn = jnp.einsum(
        "chqk,ckhd->cqhd", probs_b, v_four, preferred_element_type=jnp.float32
    ).astype(jnp.bfloat16)
    return (attn.reshape(q_blk.shape), probs, probs_b)


def attend_back(q_blk, k_blk, v_blk, probs, probs_b, attn, d_blk):
    q_four, k_four, v_four = (split_heads(q_blk), split_heads(k_blk), split_heads(v_blk))
    d_four, a_four = (split_heads(d_blk), split_heads(attn))
    grad_value = jnp.einsum(
        "chqk,cqhd->ckhd", probs_b, d_four, preferred_element_type=jnp.float32
    ).astype(jnp.bfloat16)
    grad_prob = jnp.einsum("cqhd,ckhd->chqk", d_four, v_four, preferred_element_type=jnp.float32)
    delta_row = jnp.sum(d_four.astype(jnp.float32) * a_four.astype(jnp.float32), axis=-1)
    grad_score = (probs * (grad_prob - jnp.transpose(delta_row, (0, 2, 1))[..., None])).astype(
        jnp.bfloat16
    )
    grad_qhat = jnp.einsum(
        "chqk,ckhd->cqhd", grad_score, k_four, preferred_element_type=jnp.float32
    ) / math.sqrt(HD)
    grad_khat = jnp.einsum(
        "chqk,cqhd->ckhd", grad_score, q_four, preferred_element_type=jnp.float32
    ) / math.sqrt(HD)
    shape = q_blk.shape
    return (
        grad_qhat.astype(jnp.bfloat16).reshape(shape),
        grad_khat.astype(jnp.bfloat16).reshape(shape),
        grad_value.reshape(shape),
    )


def per_device_slots(queries, key_rows, value_rows, cotangent, w_out, cluster_ids):
    token_count = queries.shape[1]
    features = queries.shape[2]
    seq_devices = lax.axis_size("seq")
    data_devices = lax.axis_size("dp")
    capacity = 2 * token_count // (CL_DEV * seq_devices)
    total_slots = 2 * token_count
    labels = cluster_ids[0]
    positions = jnp.arange(token_count)
    matching = labels[:, None] == labels[None, :]
    earlier = positions[None, :] < positions[:, None]
    ranks = jnp.sum(jnp.logical_and(matching, earlier), axis=1)
    slot_index = labels * capacity + ranks

    def pack(matrix):
        empty = jnp.zeros((total_slots, matrix.shape[1]), matrix.dtype)
        return (
            empty.at[slot_index].set(matrix).reshape(seq_devices, CL_DEV, capacity, matrix.shape[1])
        )

    def unpack(returned):
        return returned.reshape(total_slots, -1)[slot_index]

    taken_slots = (
        jnp.zeros((total_slots,), jnp.bfloat16)
        .at[slot_index]
        .set(1.0)
        .reshape(seq_devices, CL_DEV, capacity)
    )
    q_norm, q_factor = head_norm(queries[0])
    k_norm, k_factor = head_norm(key_rows[0])
    q_hat = q_norm.reshape(token_count, features).astype(jnp.bfloat16)
    k_hat = k_norm.reshape(token_count, features).astype(jnp.bfloat16)
    cotan = cotangent[0]
    w_full = lax.all_gather(w_out, "dp", axis=0, tiled=True)
    received = (
        lax.all_to_all(pack(q_hat), "seq", split_axis=0, concat_axis=2, tiled=True),
        lax.all_to_all(pack(k_hat), "seq", split_axis=0, concat_axis=2, tiled=True),
        lax.all_to_all(pack(value_rows[0]), "seq", split_axis=0, concat_axis=2, tiled=True),
        lax.all_to_all(taken_slots, "seq", split_axis=0, concat_axis=2, tiled=True),
    )
    q_blk, k_blk, v_blk = (received[0][0], received[1][0], received[2][0])
    key_valid = received[3][0] > 0
    attn_blk, probs, probs_b = attend(q_blk, k_blk, v_blk, key_valid)
    attn_back = lax.all_to_all(attn_blk[None], "seq", split_axis=2, concat_axis=0, tiled=True)
    attn = unpack(attn_back)
    grad_attn = lax.dot_general(
        cotan, w_full, (((1,), (1,)), ((), ())), preferred_element_type=jnp.float32
    ).astype(jnp.bfloat16)
    grad_recv = lax.all_to_all(pack(grad_attn), "seq", split_axis=0, concat_axis=2, tiled=True)
    grad_qblk, grad_kblk, grad_vblk = attend_back(
        q_blk, k_blk, v_blk, probs, probs_b, attn_blk, grad_recv[0]
    )
    grads_back = (
        lax.all_to_all(grad_qblk[None], "seq", split_axis=2, concat_axis=0, tiled=True),
        lax.all_to_all(grad_kblk[None], "seq", split_axis=2, concat_axis=0, tiled=True),
        lax.all_to_all(grad_vblk[None], "seq", split_axis=2, concat_axis=0, tiled=True),
    )
    grad_qhat, grad_khat, grad_values = (
        unpack(grads_back[0]),
        unpack(grads_back[1]),
        unpack(grads_back[2]),
    )
    projected = jnp.dot(attn, w_full, preferred_element_type=jnp.float32).astype(jnp.bfloat16)
    grad_queries = norm_back(grad_qhat, q_norm, q_factor).astype(jnp.bfloat16)
    grad_keys = norm_back(grad_khat, k_norm, k_factor).astype(jnp.bfloat16)
    local_term = lax.dot_general(
        attn, cotan, (((0,), (0,)), ((), ())), preferred_element_type=jnp.float32
    )
    summed = lax.psum_scatter(local_term, ("seq", "dp"), scatter_dimension=0, tiled=True)
    weight_grad = summed / math.sqrt(token_count * seq_devices * data_devices)
    return (projected[None], grad_queries[None], grad_keys[None], grad_values[None], weight_grad)


def greet_all(seq_devices):
    barrier = pltpu.get_barrier_semaphore()
    me = lax.axis_index("seq") * 2 + lax.axis_index("dp")
    everyone = 2 * seq_devices

    def greet(step, carry):
        peer = lax.rem(me + step, everyone)
        pl.semaphore_signal(
            barrier, inc=1, device_id=(peer // 2, lax.rem(peer, 2)), device_id_type=MESH
        )
        return carry

    lax.fori_loop(1, everyone, greet, 0)
    pl.semaphore_wait(barrier, everyone - 1)


def remote(source, target, sent, landed, device):
    return pltpu.make_async_remote_copy(
        src_ref=source,
        dst_ref=target,
        send_sem=sent,
        recv_sem=landed,
        device_id=device,
        device_id_type=MESH,
    )


def normalize(rows):
    wide = rows.astype(jnp.float32)
    factor = lax.rsqrt(jnp.mean(wide * wide, axis=-1, keepdims=True) + EPS)
    return wide * factor, factor


def lanes(head):
    return pl.ds(pl.multiple_of(head * HD, HD), HD)


def dispatch_kernel(
    heads, q_in, k_in, v_in, c_in, w_ref, ids_ref, full_ref, slots_ref, w_full_ref, x_ref,
    q_ref, k_ref, v_ref, c_ref, loaded, sent, landed, relay_sent, relay_landed, id_sent, id_landed, w_sent, w_landed,
):
    seq_devices = 2 * heads
    chip, core = lax.axis_index("seq"), lax.axis_index("dp")
    other = 1 - core
    seq_here, head_here = chip // heads, lax.rem(chip, heads)
    half = x_ref.shape[2]
    per_core = heads // 2
    pairs = ((q_in, q_ref), (k_in, k_ref), (v_in, v_ref), (c_in, c_ref), (w_ref, w_full_ref.at[core]))
    loads = [
        pltpu.make_async_copy(source, target, loaded.at[i])
        for i, (source, target) in enumerate(pairs)
    ]
    for load in loads:
        load.start()
    greet_all(seq_devices)
    w_copy = remote(w_ref, w_full_ref.at[core], w_sent, w_landed, (chip, other))
    w_copy.start()
    for load in loads:
        load.wait()

    def target(step):
        part = lax.rem(step, 2)
        head = lax.rem(chip + step // 2, heads)
        return part, head, core * heads + head

    def data_copy(step):
        part, head, owner = target(step)
        return remote(
            x_ref.at[head, part],
            full_ref.at[chip, part],
            sent.at[step],
            landed.at[chip],
            (owner, part),
        )

    def id_copy(step):
        part, head, owner = target(step)
        return remote(
            ids_ref, slots_ref.at[chip], id_sent.at[step], id_landed.at[chip], (owner, part)
        )

    def to_self(step):
        part, head, owner = target(step)
        return jnp.logical_and(owner == chip, part == core)

    def send(step):
        part, head, owner = target(step)

        @pl.when(jnp.logical_not(to_self(step)))
        def _():
            id_copy(step).start()
            data_copy(step).start()

        @pl.when(to_self(step))
        def _():
            full_ref[chip, part] = x_ref[head, part]
            slots_ref[chip] = ids_ref[...]

    def fill(head, index, rows):
        for part in range(2):
            x_ref[head, part, :, index * HD : (index + 1) * HD] = rows[
                part * half : (part + 1) * half
            ].astype(x_ref.dtype)

    def prepare(step, carry):
        head = lax.rem(chip + step, heads)
        fill(head, 0, normalize(q_ref[:, lanes(head)])[0])
        fill(head, 1, normalize(k_ref[:, lanes(head)])[0])
        fill(head, 2, v_ref[:, lanes(head)])

        @pl.when(step == 0)
        def _():
            remote(w_ref, w_full_ref.at[other], w_sent, w_landed, (chip, other)).wait_recv()

        w_rows = w_full_ref[head // per_core, lanes(lax.rem(head, per_core)), :]
        grad = lax.dot_general(
            c_ref[...], w_rows, (((1,), (1,)), ((), ())), preferred_element_type=jnp.float32
        )
        fill(head, 3, grad)
        send(2 * step)
        send(2 * step + 1)
        return carry

    lax.fori_loop(0, heads, prepare, 0)

    def relay_copy(source):
        return remote(
            full_ref.at[source, core],
            full_ref.at[source, core],
            relay_sent.at[source],
            relay_landed.at[source],
            (chip, other),
        )

    def receive(step, carry):
        source = lax.rem(head_here - step // 2 + heads, heads) + heads * lax.rem(step, 2)

        @pl.when(jnp.logical_not(jnp.logical_and(source == chip, seq_here == core)))
        def _():
            remote(
                x_ref.at[0, 0],
                full_ref.at[source, core],
                sent.at[0],
                landed.at[source],
                (chip, other),
            ).wait_recv()
            remote(
                ids_ref, slots_ref.at[source], id_sent.at[0], id_landed.at[source], (chip, other)
            ).wait_recv()

        relay_copy(source).start()
        return carry

    lax.fori_loop(0, seq_devices, receive, 0)

    def finish(step, carry):
        remote(
            full_ref.at[step, core],
            full_ref.at[step, other],
            relay_sent.at[step],
            relay_landed.at[step],
            (chip, other),
        ).wait_recv()
        relay_copy(step).wait_send()

        @pl.when(jnp.logical_not(to_self(step)))
        def _():
            id_copy(step).wait_send()
            data_copy(step).wait_send()

        return carry

    lax.fori_loop(0, seq_devices, finish, 0)
    w_copy.wait_send()


def dispatch_call(q, k, v, c, w, ids):
    tokens, features = q.shape
    heads = features // HD
    half, width = tokens // 2, 4 * HD
    n = 2 * heads
    vmem = pl.BlockSpec(memory_space=pltpu.VMEM)
    return pl.pallas_call(
        functools.partial(dispatch_kernel, heads),
        out_shape=(
            jax.ShapeDtypeStruct((n, 2, half, width), q.dtype),
            jax.ShapeDtypeStruct((n,) + ids.shape, ids.dtype),
            jax.ShapeDtypeStruct((2,) + w.shape, w.dtype),
        ),
        in_specs=[pl.BlockSpec(memory_space=pltpu.HBM)] * 5 + [vmem],
        out_specs=(vmem,) * 3,
        scratch_shapes=[pltpu.VMEM((heads, 2, half, width), q.dtype)]
        + [pltpu.VMEM(q.shape, q.dtype)] * 3
        + [pltpu.VMEM(c.shape, c.dtype), pltpu.SemaphoreType.DMA((5,))]
        + [pltpu.SemaphoreType.DMA((n,))] * 6
        + [pltpu.SemaphoreType.DMA] * 2,
        compiler_params=pltpu.CompilerParams(
            collective_id=0, has_side_effects=True, vmem_limit_bytes=40 << 20
        ),
    )(q, k, v, c, w, ids)


def collector(heads, t_ref, mine, out_ref, held, stage, swap_sent, swap_landed, sent, landed):
    seq_devices = 2 * heads
    chip, core = lax.axis_index("seq"), lax.axis_index("dp")
    other = 1 - core
    seq_here, head_here = chip // heads, lax.rem(chip, heads)

    def peer_of(step):
        far = heads * (1 - lax.rem(step, 2))
        return lax.rem(chip + step // 2 + far, seq_devices)

    def swap(peer):
        return remote(
            t_ref.at[other, peer],
            held.at[peer],
            swap_sent.at[peer],
            swap_landed.at[peer],
            (chip, other),
        )

    def send_copy(peer):
        return remote(
            stage.at[peer],
            out_ref.at[head_here, core],
            sent.at[peer],
            landed.at[2 * head_here + core],
            (peer, seq_here),
        )

    def to_self(peer):
        return jnp.logical_and(peer == chip, seq_here == core)

    def begin(step, carry):
        swap(peer_of(step)).start()
        return carry

    def send(step, carry):
        peer = peer_of(step)
        swap(peer).wait_recv()

        @pl.when(jnp.logical_not(to_self(peer)))
        def _():
            stage[peer] = mine(peer) + held[peer]
            send_copy(peer).start()

        @pl.when(to_self(peer))
        def _():
            out_ref[head_here, core] = mine(peer) + held[peer]

        return carry

    def wait_one(step, carry):
        head, part = step // 2, lax.rem(step, 2)
        source = core * heads + head

        @pl.when(jnp.logical_not(jnp.logical_and(source == chip, part == core)))
        def _():
            remote(
                stage.at[0], out_ref.at[head, part], sent.at[0], landed.at[step], (chip, other)
            ).wait_recv()

        swap(step).wait_send()

        @pl.when(jnp.logical_not(to_self(step)))
        def _():
            send_copy(step).wait_send()

        return carry

    return (
        lambda: lax.fori_loop(0, seq_devices, begin, 0),
        lambda low, high: lax.fori_loop(low, high, send, 0),
        wait_one,
    )


def final_kernel(
    heads, scale, t_ref, t_attn, q_ref, k_ref, c_ref, proj_ref,
    gq_ref, gk_ref, gv_ref, out_ref, grad_ref,
    own, own_loaded, got, held, stage, got_attn, held_attn, stage_attn, a_ref, w_ref, w_held, kept, x_stage, x_got, y_stage, y_got, z_stage, z_got,
    swap_sent, swap_landed, sent, landed, w_swap_sent, w_swap_landed,
    attn_swap_sent, attn_swap_landed, attn_sent, attn_landed,
    x_sent, x_landed, y_sent, y_landed, z_sent, z_landed,
):
    seq_devices = 2 * heads
    quarter = seq_devices // 4
    chip, core = lax.axis_index("seq"), lax.axis_index("dp")
    other = 1 - core
    x, y, z = lax.rem(chip, 2), lax.rem(chip // 2, 2), chip // 4
    half = got.shape[2]
    start_swaps, send_all, wait_one = collector(
        heads, t_ref, lambda peer: own[peer], got, held, stage, swap_sent, swap_landed, sent, landed
    )
    start_attn, send_attn, wait_attn = collector(
        heads, t_attn, lambda peer: t_attn[core, peer], got_attn, held_attn, stage_attn,
        attn_swap_sent, attn_swap_landed, attn_sent, attn_landed,
    )
    load = pltpu.make_async_copy(t_ref.at[core], own, own_loaded)
    load.start()
    greet_all(seq_devices)

    def w_swap(peer):
        return remote(
            w_ref.at[peer, other],
            w_held.at[peer],
            w_swap_sent.at[peer],
            w_swap_landed.at[peer],
            (chip, other),
        )

    def x_copy(j):
        return remote(
            x_stage.at[j], x_got.at[j], x_sent.at[j], x_landed.at[j], (chip + 1 - 2 * x, core)
        )

    def y_copy(j):
        return remote(
            y_stage.at[j], y_got.at[j], y_sent.at[j], y_landed.at[j], (chip + 2 - 4 * y, core)
        )

    def z_copy(j):
        return remote(
            z_stage.at[j], z_got.at[z], z_sent.at[j], z_landed.at[z], (4 * j + 2 * y + x, core)
        )

    def both_cores(peer):
        w_swap(peer).wait_recv()
        return w_ref[peer, core].astype(jnp.float32) + w_held[peer].astype(jnp.float32)

    piece = w_ref.shape[2]

    def term(head, carry):
        total = None
        for part in range(2):
            wait_attn(2 * head + part, 0)
            rows = slice(part * half, (part + 1) * half)
            block = got_attn[head, part]
            a_ref[rows, lanes(head)] = block
            partial = lax.dot_general(
                block, c_ref[rows, :], (((0,), (0,)), ((), ())), preferred_element_type=jnp.float32
            )
            total = partial if total is None else total + partial
        for index in range(4):
            w_ref[2 * head + index // 2, index % 2] = total[
                index * piece : (index + 1) * piece
            ].astype(w_ref.dtype)
        w_swap(2 * head).start()
        w_swap(2 * head + 1).start()
        return carry

    def x_phase(j, carry):
        x_stage[j] = both_cores(2 * j + 1 - x).astype(x_stage.dtype)
        x_copy(j).start()
        kept[j] = both_cores(2 * j + x)
        return carry

    def y_phase(j, carry):
        away, here = 2 * j + 1 - y, 2 * j + y
        x_copy(away).wait_recv()
        y_stage[j] = (kept[away] + x_got[away].astype(jnp.float32)).astype(y_stage.dtype)
        y_copy(j).start()
        x_copy(here).wait_recv()
        kept[here] += x_got[here].astype(jnp.float32)
        return carry

    def z_phase(j, carry):
        y_copy(j).wait_recv()
        total = kept[2 * j + y] + y_got[j].astype(jnp.float32)

        @pl.when(j != z)
        def _():
            z_stage[j] = total.astype(z_stage.dtype)
            z_copy(j).start()

        @pl.when(j == z)
        def _():
            grad_ref[...] = total

        return carry

    def z_sum(j, carry):
        @pl.when(j != z)
        def _():
            remote(
                z_stage.at[j], z_got.at[j], z_sent.at[j], z_landed.at[j], (4 * j + 2 * y + x, core)
            ).wait_recv()
            grad_ref[...] += z_got[j].astype(jnp.float32)
            z_copy(j).wait_send()

        y_copy(j).wait_send()
        return carry

    def ends(j, carry):
        x_copy(j).wait_send()
        w_swap(2 * j).wait_send()
        w_swap(2 * j + 1).wait_send()
        return carry

    start_attn()
    start_swaps()
    send_attn(0, seq_devices)
    load.wait()
    send_all(0, heads)
    lax.fori_loop(0, heads, term, 0)
    lax.fori_loop(0, seq_devices // 2, x_phase, 0)
    send_all(heads, seq_devices)
    lax.fori_loop(0, quarter, y_phase, 0)
    lax.fori_loop(0, quarter, z_phase, 0)

    depth = proj_ref.shape[1]
    tile = 2 * HD

    def project(step, carry):
        columns = pl.ds(pl.multiple_of(step * tile, tile), tile)
        total = jnp.dot(
            a_ref[:, :depth], proj_ref[0, :, columns], preferred_element_type=jnp.float32
        ) + jnp.dot(a_ref[:, depth:], proj_ref[1, :, columns], preferred_element_type=jnp.float32)
        out_ref[:, columns] = total.astype(out_ref.dtype)
        return carry

    lax.fori_loop(0, out_ref.shape[1] // tile, project, 0)

    def finish(step, carry):
        wait_one(step, carry)
        head, part = step // 2, lax.rem(step, 2)
        rows = pl.ds(pl.multiple_of(part * half, half), half)
        for index, (source, target) in enumerate(((q_ref, gq_ref), (k_ref, gk_ref))):
            normed, factor = normalize(source[rows, lanes(head)])
            gradient = got[head, part, :, index * HD : (index + 1) * HD].astype(jnp.float32)
            inner = jnp.mean(gradient * normed, axis=-1, keepdims=True)
            target[rows, lanes(head)] = (factor * (gradient - normed * inner)).astype(target.dtype)
        gv_ref[rows, lanes(head)] = got[head, part, :, 2 * HD :]
        return carry

    lax.fori_loop(0, seq_devices, finish, 0)
    lax.fori_loop(0, quarter, z_sum, 0)
    grad_ref[...] = grad_ref[...] * scale
    lax.fori_loop(0, seq_devices // 2, ends, 0)


def final_call(heads, scale, rows, attn_rows, q, k, cotan, w_full):
    _, n, half, width = rows.shape
    vmem = pl.BlockSpec(memory_space=pltpu.VMEM)
    piece = (q.shape[1] // (2 * n), w_full.shape[2])
    kind = rows.dtype
    args = (rows, attn_rows, q, k, cotan, w_full)
    like = jax.ShapeDtypeStruct(q.shape, kind)
    projected = jax.ShapeDtypeStruct((q.shape[0], w_full.shape[2]), kind)
    counts = [n] * 10 + [n // 2] * 2 + [n // 4] * 4
    return pl.pallas_call(
        functools.partial(final_kernel, heads, scale),
        out_shape=(like, like, like, projected, jax.ShapeDtypeStruct(piece, jnp.float32)),
        in_specs=[pl.BlockSpec(memory_space=pl.ANY)] + [vmem] * 5,
        out_specs=(vmem,) * 5,
        scratch_shapes=[
            pltpu.VMEM((n, half, width), kind),
            pltpu.SemaphoreType.DMA,
            pltpu.VMEM((heads, 2, half, width), kind),
            pltpu.VMEM((n, half, width), kind),
            pltpu.VMEM((n, half, width), kind),
            pltpu.VMEM((heads, 2, half, HD), kind),
            pltpu.VMEM((n, half, HD), kind),
            pltpu.VMEM((n, half, HD), kind),
            pltpu.VMEM(q.shape, kind),
            pltpu.VMEM((n, 2) + piece, kind),
            pltpu.VMEM((n,) + piece, kind),
            pltpu.VMEM((n // 2,) + piece, jnp.float32),
            pltpu.VMEM((n // 2,) + piece, kind),
            pltpu.VMEM((n // 2,) + piece, kind),
        ]
        + [pltpu.VMEM((n // 4,) + piece, kind)] * 4
        + [pltpu.SemaphoreType.DMA((count,)) for count in counts],
        compiler_params=pltpu.CompilerParams(
            collective_id=2, has_side_effects=True, vmem_limit_bytes=48 << 20
        ),
    )(*args)


def per_device_heads(queries, key_rows, value_rows, cotangent, w_out, cluster_ids):
    tokens, features = queries.shape[1], queries.shape[2]
    heads = features // HD
    seq_devices = lax.axis_size("seq")
    half = tokens // 2
    clusters = CL_DEV * seq_devices
    capacity = 2 * tokens // clusters
    core = lax.axis_index("dp")
    labels = cluster_ids[0]
    positions = jnp.arange(tokens)
    matching = labels[:, None] == labels[None, :]
    earlier = positions[None, :] < positions[:, None]
    ranks = jnp.sum(jnp.logical_and(matching, earlier), axis=1)
    slot_index = (labels * capacity + ranks).astype(jnp.int32)
    ids = slot_index.reshape(2, half)

    cotan = cotangent[0]
    width = 4 * HD
    full, landed_ids, w_full = dispatch_call(
        queries[0], key_rows[0], value_rows[0], cotan, w_out, ids
    )
    slots = landed_ids.reshape(seq_devices, tokens)
    my_slots = clusters * capacity // 2
    wanted = core * my_slots + jnp.arange(my_slots)
    one_hot = (slots[:, None, :] == wanted[None, :, None]).astype(jnp.bfloat16)
    packed = jnp.einsum(
        "dst,dtf->dsf",
        one_hot,
        full.reshape(seq_devices, tokens, width),
        preferred_element_type=jnp.float32,
    ).astype(jnp.bfloat16)
    packed = packed.reshape(seq_devices, clusters // 2, capacity, width)
    packed = jnp.transpose(packed, (1, 0, 2, 3))
    packed = packed.reshape(clusters // 2, seq_devices * capacity, width)
    q_blk, k_blk, v_blk, d_blk = [packed[:, :, i * HD : (i + 1) * HD] for i in range(4)]
    taken = jnp.sum(one_hot.astype(jnp.float32), axis=2)
    taken = taken.reshape(seq_devices, clusters // 2, capacity)
    key_valid = jnp.transpose(taken, (1, 0, 2)).reshape(clusters // 2, -1) > 0

    def take(blocks):
        count = len(blocks)
        joined = jnp.concatenate(blocks, axis=-1)
        joined = joined.reshape(clusters // 2, seq_devices, capacity, count * HD)
        joined = jnp.transpose(joined, (1, 0, 2, 3)).reshape(seq_devices, my_slots, count * HD)
        rows = jnp.einsum(
            "dspt,dsf->pdtf",
            one_hot.reshape(seq_devices, my_slots, 2, half),
            joined,
            preferred_element_type=jnp.float32,
        )
        return rows.astype(jnp.bfloat16)

    attn_blk, probs, probs_b = attend(q_blk, k_blk, v_blk, key_valid)
    grads = attend_back(q_blk, k_blk, v_blk, probs, probs_b, attn_blk, d_blk)
    scale = 1.0 / math.sqrt(tokens * seq_devices * 2)
    grad_queries, grad_keys, grad_values, projected, weight_grad = final_call(
        heads, scale, take(list(grads)), take([attn_blk]), queries[0], key_rows[0], cotan, w_full
    )
    return (projected[None], grad_queries[None], grad_keys[None], grad_values[None], weight_grad)


def per_device(queries, *rest):
    heads = queries.shape[2] // HD
    if lax.axis_size("dp") == 2 and lax.axis_size("seq") == 2 * heads:
        return per_device_heads(queries, *rest)
    return per_device_slots(queries, *rest)


def solution(mesh):
    in_specs = (
        P("dp", "seq", None),
        P("dp", "seq", None),
        P("dp", "seq", None),
        P("dp", "seq", None),
        P("dp", None),
        P("dp", "seq"),
    )
    out_specs = (
        P("dp", "seq", None),
        P("dp", "seq", None),
        P("dp", "seq", None),
        P("dp", "seq", None),
        P(("seq", "dp"), None),
    )
    return jax.shard_map(
        per_device, mesh=mesh, in_specs=in_specs, out_specs=out_specs, check_vma=False
    )
```
